512 devices in a mesh: mem: 8 (over y, core), gy: 4 (over z_hi), gx: 16 (over x, z_lo).
Axes of the slice: x: 4, y: 4, z: 16 (z_hi: 4, z_lo: 4; z = z_hi * 4 + z_lo), core: 2. Of those that a mesh axis runs over, the one named last changes fastest.
Arguments:
- perturbations: bfloat16 [16, 5, 16, 32, 2048], P('mem', None, None, 'gy', 'gx'), may hold values from -6 to 6
- control: float32 [16, 16, 32, 2048], P('mem', None, 'gy', 'gx'), may hold values from -6 to 6
- background: float32 [5, 16, 32, 2048], P(None, 'mem', 'gy', 'gx'), may hold values from -6 to 6
- obs_cell: int32 [128, 2048], P('gy', 'gx'), may hold values from 0 to 81919
- huber_flag: int32 [128, 2048], P('gy', 'gx'), may hold values 0 or 1
- innovation: float32 [128, 2048], P('gy', 'gx'), may hold values from -6 to 6
- precision: float32 [128, 2048], P('gy', 'gx'), may hold values from 10 to 100
Outputs:
- analysis: float32 [5, 16, 32, 2048], P(None, 'mem', 'gy', 'gx')
- control_out: float32 [16, 16, 32, 2048], P('mem', None, 'gy', 'gx')
The draws below stay inside these ranges and needn't reach their ends.
Inputs may be any that keep to these rules, and one draw needn't show every extreme that they name: `obs_cell`: a cell of its tile, ordered by variable, then level, then row, then column.
All inputs are finite; a program needn't handle non-finite values. No bound on the sum of `huber_flag` on one device may be relied on, other than what follows from the above.
Results may differ from the reference program's by a relative error of at most 0.0003.
Values sent between devices are 32-bit elements; how exact they have to be, the bound alone decides.
A program may use at most 64 MiB of HBM per device.

```python
import math
import jax
import jax.numpy as jnp
from jax import lax

VARS = 5
NZ = 16
TY = 8
TX = 128
OBS_R = 32
OBS_C = 128
ITERS = 2
MEMBERS = 16
NY = 32
NX = 2048
NOBSY = 128
NOBSX = 2048


def place_ends(drawn, stream_key, smallest, largest):
    shape = drawn.shape
    spot = [jax.random.randint(jax.random.fold_in(stream_key, axis), (), 0, shape[axis]) for axis in range(len(shape))]
    drawn = drawn.at[tuple(spot)].set(smallest)
    longest = shape.index(max(shape))
    spot[longest] = (spot[longest] + 1) % shape[longest]
    return drawn.at[tuple(spot)].set(largest)


def with_spikes(result, own_key, source, target, blocks, factor):
    owner, partner = [(jnp.arange(result.shape[axis_at]) // (result.shape[axis_at] // blocks)).reshape([-1 if axis == axis_at else 1 for axis in range(result.ndim)]) for axis_at in (source, target)]
    chosen = jax.random.permutation(own_key, blocks)[partner]
    strong = (owner == chosen) | (owner == (partner + blocks // 2) % blocks)
    return jnp.where(strong, factor * result, result)


def shard_levels(stream_key, shape, shards, low, high):
    factor_of, own = 1.0, jax.random.fold_in(stream_key, 6)
    for dim, parts in shards:
        heights = jnp.exp(jax.random.uniform(jax.random.fold_in(own, dim), (parts,), jnp.float32, low / len(shards), high / len(shards)))
        factor_of = factor_of * jnp.repeat(heights, shape[dim] // parts).reshape([-1 if axis == dim else 1 for axis in range(len(shape))])
    return factor_of


def bell_draw(own_key, dims, scale, most, cuts=(), held_as=jnp.bfloat16):
    drawn = jax.random.normal(own_key, dims, jnp.float32) * scale
    if len(cuts) > 0:
        drawn = shard_levels(own_key, dims, cuts, -0.22, 0.18) * drawn
    return jnp.clip(drawn, min=-most, max=most).astype(held_as)


def bell_draw_with(stream_key, shape, deviation, reach, split, heavy, dtype=jnp.bfloat16):
    drawn = deviation * jax.random.normal(stream_key, shape, jnp.float32)
    if split:
        drawn = drawn * shard_levels(stream_key, shape, split, -0.22, 0.18)
    return jnp.clip(with_spikes(drawn, jax.random.fold_in(stream_key, 3), *heavy), -reach, reach).astype(dtype)


def setup_inputs(seed: int = 0) -> dict:
    splits = jax.random.split(jax.random.key(seed), 8)
    return {
        "perturbations": bell_draw_with(splits[0], (MEMBERS, VARS, NZ, NY, NX), 1.0, 6.0, ((0, 8), (3, 4), (4, 16)), (0, 2, 8, 2.0)),
        "control": bell_draw(splits[1], (MEMBERS, NZ, NY, NX), 1.0, 6.0, ((0, 8), (2, 4), (3, 16)), jnp.float32),
        "background": bell_draw(splits[2], (VARS, NZ, NY, NX), 1.0, 6.0, ((1, 8), (2, 4), (3, 16)), jnp.float32),
        "obs_cell": place_ends(jax.random.randint(splits[3], (NOBSY, NOBSX), 0, VARS * NZ * TY * TX), jax.random.fold_in(splits[3], 1), 0, (VARS * NZ * TY * TX) - 1).astype(jnp.int32),
        "huber_flag": place_ends((jax.random.randint(splits[4], (NOBSY, NOBSX), 0, 3) < 1).astype(jnp.int32), jax.random.fold_in(splits[4], 1), 0, 1),
        "innovation": bell_draw(splits[5], (NOBSY, NOBSX), 1.0, 6.0, ((0, 4), (1, 16)), jnp.float32),
        "precision": jnp.clip(jnp.exp(math.log(100.0) - 2.3025851 * jax.random.uniform(splits[6], (NOBSY, NOBSX), jnp.float32) ** shard_levels(splits[6], (NOBSY, NOBSX), ((0, 4), (1, 16)), -0.2, 0.2)), 10.0, 100.0),
    }


huber_width = 1.0

def filter_taps():
    offsets = jnp.arange(-4, 5).astype(jnp.float32)
    raw = jnp.exp(-offsets * offsets / 8.0)
    return raw / jnp.sum(raw)

def smooth(field):
    weights = filter_taps()
    rows, cols = (field.shape[-2], field.shape[-1])
    widths = [(0, 0)] * (field.ndim - 2) + [(4, 4), (4, 4)]
    padded = jnp.pad(field, widths)
    along = sum((weights[offset] * padded[..., :, offset:offset + cols] for offset in range(9)))
    return sum((weights[offset] * along[..., offset:offset + rows, :] for offset in range(9)))

def member_sum(perturbations, alpha):

    def add_one(total, member_pair):
        member_pert, member_field = member_pair
        return (total + member_pert.astype(jnp.float32) * member_field[None], None)
    start = jnp.zeros(perturbations.shape[1:], jnp.float32)
    total, unused = lax.scan(add_one, start, (perturbations, alpha))
    return total

def project(perturbations, adjoint):
    return lax.map(lambda member_pert: lax.optimization_barrier(jnp.sum(member_pert.astype(jnp.float32) * adjoint, axis=0)), perturbations)

def reference(perturbations, control, background, obs_cell, huber_flag, innovation, precision):
    cells = TY * TX
    var_of = obs_cell // (NZ * cells)
    rest = obs_cell % (NZ * cells)
    level = rest // cells
    spot = rest % cells
    tile_row = (jnp.arange(obs_cell.shape[0]).astype(jnp.int32) // OBS_R)[:, None]
    tile_col = (jnp.arange(obs_cell.shape[1]).astype(jnp.int32) // OBS_C)[None, :]
    grid_row = (tile_row * TY + spot // TX).astype(jnp.int32)
    grid_col = (tile_col * TX + spot % TX).astype(jnp.int32)
    state = control
    increment = member_sum(perturbations, smooth(state))
    for iteration in range(ITERS):
        misfit = increment[var_of, level, grid_row, grid_col] - innovation
        scaled = misfit / huber_width
        weight = jnp.where(huber_flag == 1, 1.0 / jnp.sqrt(1.0 + scaled * scaled), 1.0)
        adjoint = jnp.zeros_like(increment).at[var_of, level, grid_row, grid_col].add(precision * weight * misfit)
        grad = state + smooth(project(perturbations, adjoint))
        delta = member_sum(perturbations, smooth(grad))
        grad_norm = jnp.sum(grad * grad)
        seen_step = delta[var_of, level, grid_row, grid_col]
        curv = jnp.sum(precision * weight * seen_step * seen_step)
        step = grad_norm / (grad_norm + curv)
        state = state - step * grad
        increment = increment - step * delta
    return (background + increment, state)
```

```python
import functools

import jax
import jax.numpy as jnp
import numpy as np
from jax import lax
from jax.experimental import pallas as pl
from jax.experimental.pallas import tpu as pltpu
from jax.sharding import PartitionSpec as P

MESH = pl.DeviceIdType.MESH
F32, BF16 = jnp.float32, jnp.bfloat16
MEM, GY, GX = 8, 4, 16
TILES = GY * GX
ITERS = 2
CHUNKS = 8
UP, OWN, DN = 0, 1, 2
LF, RT = 0, 1


def taps():
    offsets = np.arange(-4, 5).astype(np.float32)
    raw = np.exp(-offsets * offsets / np.float32(8.0))
    return (raw / raw.sum()).astype(np.float64)


def one_axis(length):
    weights = taps()
    distance = np.arange(length)[None, :] - np.arange(length)[:, None]
    inside = np.abs(distance) <= 4
    once = np.where(inside, weights[np.clip(distance + 4, 0, 8)], 0.0)
    return once, once @ once


def window(full, first_in, rows, first_out, cols):
    out = np.zeros((rows, cols))
    for i in range(rows):
        if 0 <= first_in + i < full.shape[0]:
            out[i] = full[first_in + i, first_out : first_out + cols]
    return out


def row_matrices():
    once, twice = one_axis(GY * 8)
    eye16, eye32 = np.eye(16), np.eye(32)
    ky = np.zeros((GY, 384, 256))
    kv = np.zeros((GY, 512, 256))
    for g in range(GY):
        for t in range(3):
            first = 8 * (g + t - 1)
            ky[g, t * 128 : t * 128 + 128, :128] = np.kron(eye16, window(once, first, 8, 8 * g, 8))
            ky[g, t * 128 : t * 128 + 128, 128:] = np.kron(eye16, window(twice, first, 8, 8 * g, 8))
        kv[g, :256] = np.kron(eye32, window(once, 8 * g, 8, 8 * g, 8))
        kv[g, 256:384] = np.kron(eye32, window(once, 8 * g - 4, 4, 8 * g, 8))
        kv[g, 384:] = np.kron(eye32, window(once, 8 * g + 8, 4, 8 * g, 8))
    return ky.astype(np.float32), kv.astype(np.float32)


def column_matrices():
    length = 128 * 3
    weights = one_axis(length)
    kx = np.zeros((3, 256, 256))
    for place, first in enumerate((0, 128, 256)):
        for k in range(2):
            rows = slice(k * 128, k * 128 + 128)
            kx[place, rows, :128] = window(weights[k], first, 128, first, 128).T
            kx[place, rows, 128:136] = window(weights[k], first - 8, 8, first, 128).T
            kx[place, rows, 136:144] = window(weights[k], first + 128, 8, first, 128).T
    return kx.astype(np.float32)


def row_selection():
    top = np.kron(np.eye(32), np.eye(8)[:, :4])
    bottom = np.kron(np.eye(32), np.eye(8)[:, 4:])
    return np.concatenate([top, bottom], axis=1).astype(np.float32)


def mm(a, b):
    return jnp.dot(a, b, preferred_element_type=F32, precision=lax.Precision.HIGHEST)


def halves(x):
    hi = x.astype(BF16)
    return hi, (x - hi.astype(F32)).astype(BF16)


def build_onehot(cell, onehot, t):
    index = lax.broadcasted_iota(jnp.int32, (512, 128), 0)

    def body(c, carry):
        for k in range(4):
            row = cell[t, pl.ds(c * 4 + k, 1), :]
            key = ((row & 127) >> 5) * 128 + ((row >> 7) & 127)
            onehot[t, c, :, k * 128 : k * 128 + 128] = jnp.where(index == key, 1.0, 0.0).astype(BF16)
        return carry

    lax.fori_loop(0, CHUNKS, body, 0)


def pert_at_obs(pert, table, cell, onehot, po):
    for v in range(5):
        for m in range(2):
            block = pert[(m * 5 + v) * 128 : (m * 5 + v + 1) * 128, :].astype(F32).T.astype(BF16)
            for xq in range(4):
                table[(v * 2 + m) * 32 : (v * 2 + m + 1) * 32, xq * 128 : xq * 128 + 128] = block[xq * 32 : xq * 32 + 32]
    index = lax.broadcasted_iota(jnp.int32, (32, 128), 0)

    def body(c, carry):
        got = jnp.dot(table[...], onehot[OWN, c], preferred_element_type=F32)
        for k in range(4):
            row = cell[OWN, pl.ds(c * 4 + k, 1), :]
            key = (row >> 14) * 32 + (row & 31)
            lanes = slice(k * 128, k * 128 + 128)
            for m in range(2):
                acc = jnp.zeros((32, 128), F32)
                for v in range(5):
                    acc = jnp.where(index + 32 * v == key, got[(v * 2 + m) * 32 : (v * 2 + m + 1) * 32, lanes], acc)
                po[OWN, m, pl.ds(c * 4 + k, 1), :] = jnp.sum(acc, axis=0, keepdims=True)
        return carry

    lax.fori_loop(0, CHUNKS, body, 0)


def observe(field, left, cell, onehot, po, out):
    for m in range(2):
        for xq in range(4):
            hi, lo = halves(field[xq * 32 : xq * 32 + 32, m * 128 : m * 128 + 128])
            left[m * 64 : m * 64 + 32, xq * 128 : xq * 128 + 128] = hi
            left[m * 64 + 32 : m * 64 + 64, xq * 128 : xq * 128 + 128] = lo
    index = lax.broadcasted_iota(jnp.int32, (32, 128), 0)

    def body(c, carry):
        got = jnp.dot(left[...], onehot[OWN, c], preferred_element_type=F32)
        for k in range(4):
            r = pl.ds(c * 4 + k, 1)
            lanes = slice(k * 128, k * 128 + 128)
            total = po[OWN, 0, r, :] * (got[0:32, lanes] + got[32:64, lanes])
            total += po[OWN, 1, r, :] * (got[64:96, lanes] + got[96:128, lanes])
            total = jnp.where(index == (cell[OWN, r, :] & 31), total, 0.0)
            out[r, :] = jnp.sum(total, axis=0, keepdims=True)
        return carry

    lax.fori_loop(0, CHUNKS, body, 0)


def spread(t, q, cell, onehot, po, acc, w):
    index = lax.broadcasted_iota(jnp.int32, (32, 128), 0)
    acc[...] = jnp.zeros_like(acc)

    def body(c, carry):
        columns = []
        for k in range(4):
            r = pl.ds(c * 4 + k, 1)
            mine = index == (cell[t, r, :] & 31)
            parts = []
            for m in range(2):
                value = po[t, m, r, :] * q[r, :]
                hi = value.astype(BF16).astype(F32)
                parts.append(jnp.where(mine, hi, 0.0))
                parts.append(jnp.where(mine, value - hi, 0.0))
            columns.append(jnp.concatenate(parts, axis=0).astype(BF16))
        acc[...] += lax.dot_general(
            jnp.concatenate(columns, axis=1), onehot[t, c], (((1,), (1,)), ((), ())), preferred_element_type=F32
        )
        return carry

    lax.fori_loop(0, CHUNKS, body, 0)
    for m in range(2):
        for xq in range(4):
            lanes = slice(xq * 128, xq * 128 + 128)
            w[t, m, xq * 32 : xq * 32 + 32, :] = acc[m * 64 : m * 64 + 32, lanes] + acc[m * 64 + 32 : m * 64 + 64, lanes]


def member_part(field, pert, out):
    turned = [field[:, m * 128 : m * 128 + 128].T for m in range(2)]
    for v in range(5):
        block = sum(pert[(m * 5 + v) * 128 : (m * 5 + v + 1) * 128, :].astype(F32) * turned[m] for m in range(2))
        for j in range(MEM):
            out[j, v] = block[j * 16 : j * 16 + 16]


def kernel(
    pert_in, ctrl_in, cell_in, flag_in, innov_in, prec_in, ky_in, kv_in, kx_in, sel_in,
    inc_out, change_out,
    pert, ctrl, cell, flag, innov, prec, ky, kv, kx, sel,
    onehot, table, left, acc, po, q, w,
    v_pack, v_edge, v_rows, v_strip, h_send, h_recv, w_send, w_recv, g_send, g_recv, r_send, r_recv,
    local_sem, send_sem, recv_sem,
):
    me_m, me_y, me_x = lax.axis_index("mem"), lax.axis_index("gy"), lax.axis_index("gx")
    up, dn = {"gy": lax.rem(me_y + 3, GY)}, {"gy": lax.rem(me_y + 1, GY)}
    lf, rt = {"gx": lax.rem(me_x + 15, GX)}, {"gx": lax.rem(me_x + 1, GX)}

    def member_peer(i):
        return {"mem": lax.rem(me_m + i, MEM)}

    def tile_peer(i):
        return {
            "gy": lax.rem(me_y + lax.rem(i // GX + 1, GY), GY),
            "gx": lax.rem(me_x + lax.rem(lax.rem(i, GX) + 1, GX), GX),
        }

    place = jnp.where(me_x == 0, 0, jnp.where(me_x == GX - 1, 2, 1))
    loads = [
        (ctrl_in, ctrl),
        (sel_in, sel),
        (cell_in, cell.at[OWN]),
        (pert_in, pert),
        (kv_in.at[me_y], kv),
        (kx_in.at[place], kx),
        (flag_in, flag),
        (innov_in, innov),
        (prec_in, prec),
        (ky_in.at[me_y], ky),
    ]
    loads = [pltpu.make_async_copy(src, dst, local_sem.at[i]) for i, (src, dst) in enumerate(loads)]
    for load in loads:
        load.start()

    barrier = pltpu.get_barrier_semaphore()
    for i in range(1, MEM):
        pl.semaphore_signal(barrier, inc=1, device_id=member_peer(i), device_id_type=MESH)

    def greet(i, carry):
        pl.semaphore_signal(barrier, inc=1, device_id=tile_peer(i), device_id_type=MESH)
        return carry

    lax.fori_loop(0, TILES - 1, greet, 0)

    sent = []
    used = [0]

    def copy(src, dst, device):
        i = used[0]
        used[0] += 1
        out = pltpu.make_async_remote_copy(
            src_ref=src, dst_ref=dst, send_sem=send_sem.at[i], recv_sem=recv_sem.at[i], device_id=device, device_id_type=MESH
        )
        out.start()
        sent.append(out)
        return out

    loads[0].wait()
    field = jnp.concatenate([ctrl[0:128, :].T, ctrl[128:256, :].T], axis=1)
    loads[1].wait()
    packed = mm(field, sel[...])
    v_pack[0], v_pack[1] = packed[:, :128], packed[:, 128:]
    for m in range(2):
        v_edge[0, m] = field[0:8, m * 128 : m * 128 + 128]
        v_edge[1, m] = field[120:128, m * 128 : m * 128 + 128]
    loads[2].wait()

    pl.semaphore_wait(barrier, MEM - 1 + TILES - 1)

    first, last = pl.ds(0, 8), pl.ds(120, 8)
    halo = [
        copy(v_pack.at[0], v_rows.at[1], up),
        copy(v_pack.at[1], v_rows.at[0], dn),
        copy(v_edge.at[0], v_strip.at[RT, pl.ds(0, 2)], lf),
        copy(v_edge.at[1], v_strip.at[LF, pl.ds(0, 2)], rt),
        copy(v_pack.at[0, first], v_strip.at[RT, 3], {**up, **lf}),
        copy(v_pack.at[0, last], v_strip.at[LF, 3], {**up, **rt}),
        copy(v_pack.at[1, first], v_strip.at[RT, 2], {**dn, **lf}),
        copy(v_pack.at[1, last], v_strip.at[LF, 2], {**dn, **rt}),
    ]
    cells = [copy(cell.at[OWN], cell.at[DN], up), copy(cell.at[OWN], cell.at[UP], dn)]

    build_onehot(cell, onehot, OWN)
    loads[3].wait()
    pert_at_obs(pert, table, cell, onehot, po)
    perts = [copy(po.at[OWN], po.at[DN], up), copy(po.at[OWN], po.at[UP], dn)]

    for load in loads[4:]:
        load.wait()
    rows_v = mm(field, kv[0:256])
    for one in halo:
        one.wait_recv()
    rows_v += mm(jnp.concatenate([v_rows[0], v_rows[1]], axis=1), kv[256:512])
    strips = [jnp.concatenate([v_strip[side, i] for i in range(4)], axis=1) for side in (LF, RT)]
    strips = mm(jnp.concatenate(strips, axis=0), kv[...])
    smoothed = mm(kx[0:128, 0:128], rows_v) + mm(kx[0:128, 128:144], strips)

    def sum_members(phase):
        base = used[0]
        used[0] += 1
        for i in range(1, MEM):
            pltpu.make_async_remote_copy(
                src_ref=h_send.at[phase],
                dst_ref=h_recv.at[phase, i - 1],
                send_sem=send_sem.at[base],
                recv_sem=recv_sem.at[base],
                device_id=member_peer(i),
                device_id_type=MESH,
            ).start()
        every = pltpu.make_async_copy(h_recv.at[phase], h_recv.at[phase], recv_sem.at[base])
        sent_all.append((h_recv.at[phase], base))

        def total():
            every.wait()
            out = h_send[phase]
            for i in range(MEM - 1):
                out += h_recv[phase, i]
            return out

        return total

    sent_all = []

    def share_levels(k):
        base = used[0]
        used[0] += 1
        for i in range(1, MEM):
            pltpu.make_async_remote_copy(
                src_ref=r_send.at[k, lax.rem(me_m + i, MEM)],
                dst_ref=r_recv.at[k, i - 1],
                send_sem=send_sem.at[base],
                recv_sem=recv_sem.at[base],
                device_id=member_peer(i),
                device_id_type=MESH,
            ).start()
        sent_all.append((r_recv.at[k], base))
        every = pltpu.make_async_copy(r_recv.at[k], r_recv.at[k], recv_sem.at[base])

        def total():
            every.wait()
            out = r_send[k, me_m]
            for i in range(MEM - 1):
                out += r_recv[k, i]
            return out

        return total

    observe(smoothed, left, cell, onehot, po, h_send.at[0])
    h_send[0, 32:40, :] = jnp.zeros((8, 128), F32)
    total = sum_members(0)
    for one in cells:
        one.wait_recv()
    build_onehot(cell, onehot, UP)
    build_onehot(cell, onehot, DN)
    state = field
    seen = total()[0:32]
    lane = lax.broadcasted_iota(jnp.int32, (1, 128), 1)
    levels = []
    changes = jnp.zeros_like(field)
    for it in range(ITERS):
        misfit = seen - innov[...]
        weight = jnp.where(flag[...] == 1, 1.0 / jnp.sqrt(1.0 + misfit * misfit), 1.0)
        inverse = prec[...] * weight
        q[it, OWN] = inverse * misfit
        rows = [copy(q.at[it, OWN], q.at[it, DN], up), copy(q.at[it, OWN], q.at[it, UP], dn)]
        spread(OWN, q.at[it, OWN], cell, onehot, po, acc, w)
        if it == 0:
            for one in perts:
                one.wait_recv()
        else:
            member_part(smoothed, pert, r_send.at[0])
            levels.append(share_levels(0))
        rows[1].wait_recv()
        spread(UP, q.at[it, UP], cell, onehot, po, acc, w)
        rows[0].wait_recv()
        spread(DN, q.at[it, DN], cell, onehot, po, acc, w)
        for t in range(3):
            for m in range(2):
                w_send[it, 0, t, m] = w[t, m, 0:8, :]
                w_send[it, 1, t, m] = w[t, m, 120:128, :]
        sides = [copy(w_send.at[it, 0], w_recv.at[it, RT], lf), copy(w_send.at[it, 1], w_recv.at[it, LF], rt)]
        along = sum(
            mm(jnp.concatenate([w[t, 0], w[t, 1]], axis=0), ky[t * 128 : t * 128 + 128, :]) for t in range(3)
        )
        once = mm(kx[0:128, 0:128], jnp.concatenate([along[0:128, 0:128], along[128:256, 0:128]], axis=1))
        twice = mm(kx[128:256, 0:128], jnp.concatenate([along[0:128, 128:256], along[128:256, 128:256]], axis=1))
        for one in sides:
            one.wait_recv()
        edge = sum(
            mm(
                jnp.concatenate([w_recv[it, side, t, m] for m in range(2) for side in (LF, RT)], axis=0),
                ky[t * 128 : t * 128 + 128, :],
            )
            for t in range(3)
        )
        once += mm(kx[0:128, 128:144], jnp.concatenate([edge[0:16, 0:128], edge[16:32, 0:128]], axis=1))
        twice += mm(kx[128:256, 128:144], jnp.concatenate([edge[0:16, 128:256], edge[16:32, 128:256]], axis=1))
        grad = state + once
        change = smoothed + twice
        observe(change, left, cell, onehot, po, h_send.at[it + 1])
        norm = jnp.sum((grad * grad).reshape(16, 8, 256), axis=0)
        h_send[it + 1, 32:40, :] = norm[:, 0:128] + norm[:, 128:256]
        total = sum_members(it + 1)
        if it == ITERS - 1:
            member_part(change, pert, r_send.at[1])
            levels.append(share_levels(1))
        totals = total()
        delta = totals[0:32]
        norm = jnp.sum(totals[32:40], axis=0, keepdims=True)
        curv = jnp.sum(inverse * delta * delta, axis=0, keepdims=True)
        norm = norm + pltpu.roll(norm, 64, 1)
        curv = curv + pltpu.roll(curv, 64, 1)
        both = jnp.where(lane < 64, norm, curv)
        g_send[it] = both
        base = used[0]
        used[0] += 1

        def scatter_scalars(i, carry):
            pltpu.make_async_remote_copy(
                src_ref=g_send.at[it],
                dst_ref=g_recv.at[it, i],
                send_sem=send_sem.at[base],
                recv_sem=recv_sem.at[base],
                device_id=tile_peer(i),
                device_id_type=MESH,
            ).start()
            return carry

        lax.fori_loop(0, TILES - 1, scatter_scalars, 0)
        sent_all.append((g_recv.at[it], base))
        pltpu.make_async_copy(g_recv.at[it], g_recv.at[it], recv_sem.at[base]).wait()
        both = both + jnp.sum(g_recv[it], axis=0)
        norm = jnp.sum(jnp.where(lane < 64, both, 0.0), axis=1, keepdims=True)
        curv = jnp.sum(jnp.where(lane < 64, 0.0, both), axis=1, keepdims=True)
        step = norm / (norm + curv)
        state = state - step * grad
        changes = changes + step * grad
        if it < ITERS - 1:
            smoothed = smoothed - step * change
            seen = seen - step * delta
    inc_out[...] = levels[0]() - step.reshape(1, 1, 1) * levels[1]()
    for m in range(2):
        change_out[m * 128 : m * 128 + 128, :] = changes[:, m * 128 : m * 128 + 128].T
    for one in sent:
        one.wait_send()
    for ref, i in sent_all:
        pltpu.make_async_copy(ref, ref, send_sem.at[i]).wait()


def per_device(perturbations, control, background, obs_cell, huber_flag, innovation, precision):
    ky, kv = row_matrices()
    kx, sel = column_matrices(), row_selection()
    args = (
        perturbations.reshape(1280, 128), control.reshape(256, 128), obs_cell, huber_flag, innovation, precision,
        jnp.asarray(ky), jnp.asarray(kv), jnp.asarray(kx), jnp.asarray(sel),
    )
    i32 = jnp.int32
    inc, change = pl.pallas_call(
        kernel,
        out_shape=(jax.ShapeDtypeStruct((5, 16, 128), F32), jax.ShapeDtypeStruct((256, 128), F32)),
        in_specs=[pl.BlockSpec(memory_space=pltpu.HBM)] * len(args),
        out_specs=(pl.BlockSpec(memory_space=pltpu.VMEM),) * 2,
        scratch_shapes=[
            pltpu.VMEM((1280, 128), BF16),
            pltpu.VMEM((256, 128), F32),
            pltpu.VMEM((3, 32, 128), i32),
            pltpu.VMEM((32, 128), i32),
            pltpu.VMEM((32, 128), F32),
            pltpu.VMEM((32, 128), F32),
            pltpu.VMEM((384, 256), F32),
            pltpu.VMEM((512, 256), F32),
            pltpu.VMEM((256, 256), F32),
            pltpu.VMEM((256, 256), F32),
            pltpu.VMEM((3, CHUNKS, 512, 512), BF16),
            pltpu.VMEM((320, 512), BF16),
            pltpu.VMEM((128, 512), BF16),
            pltpu.VMEM((128, 512), F32),
            pltpu.VMEM((3, 2, 32, 128), F32),
            pltpu.VMEM((ITERS, 3, 32, 128), F32),
            pltpu.VMEM((3, 2, 128, 128), F32),
            pltpu.VMEM((2, 128, 128), F32),
            pltpu.VMEM((2, 2, 8, 128), F32),
            pltpu.VMEM((2, 128, 128), F32),
            pltpu.VMEM((2, 4, 8, 128), F32),
            pltpu.VMEM((ITERS + 1, 40, 128), F32),
            pltpu.VMEM((ITERS + 1, MEM - 1, 40, 128), F32),
            pltpu.VMEM((ITERS, 2, 3, 2, 8, 128), F32),
            pltpu.VMEM((ITERS, 2, 3, 2, 8, 128), F32),
            pltpu.VMEM((ITERS, 1, 128), F32),
            pltpu.VMEM((ITERS, TILES - 1, 1, 128), F32),
            pltpu.VMEM((2, MEM, 5, 16, 128), F32),
            pltpu.VMEM((2, MEM - 1, 5, 16, 128), F32),
            pltpu.SemaphoreType.DMA((10,)),
            pltpu.SemaphoreType.DMA((32,)),
            pltpu.SemaphoreType.DMA((32,)),
        ],
        compiler_params=pltpu.CompilerParams(collective_id=0, has_side_effects=True, vmem_limit_bytes=63 * 2**20 + 2**19),
    )(*args)
    return background + inc.reshape(background.shape), control - change.reshape(control.shape)


def solution(mesh):
    grid = P("mem", None, "gy", "gx")
    table = P("gy", "gx")
    return jax.shard_map(
        per_device,
        mesh=mesh,
        in_specs=(P("mem", None, None, "gy", "gx"), grid, P(None, "mem", "gy", "gx"), table, table, table, table),
        out_specs=(P(None, "mem", "gy", "gx"), grid),
        check_vma=False,
    )
```

```python
import functools

import jax
import jax.numpy as jnp
import numpy as np
from jax import lax
from jax.experimental import pallas as pl
from jax.experimental.pallas import tpu as pltpu
from jax.sharding import PartitionSpec as P

MESH = pl.DeviceIdType.MESH
F32, BF16 = jnp.float32, jnp.bfloat16
MEM, GY, GX = 8, 4, 16
TILES = GY * GX
ITERS = 2
UP, OWN, DN = 0, 1, 2
LF, RT = 0, 1


def taps():
    offsets = np.arange(-4, 5).astype(np.float32)
    raw = np.exp(-offsets * offsets / np.float32(8.0))
    return (raw / raw.sum()).astype(np.float64)


def one_axis(length):
    weights = taps()
    distance = np.arange(length)[None, :] - np.arange(length)[:, None]
    inside = np.abs(distance) <= 4
    once = np.where(inside, weights[np.clip(distance + 4, 0, 8)], 0.0)
    return once, once @ once


def window(full, first_in, rows, first_out, cols):
    out = np.zeros((rows, cols))
    for i in range(rows):
        if 0 <= first_in + i < full.shape[0]:
            out[i] = full[first_in + i, first_out : first_out + cols]
    return out


def row_matrices():
    once, twice = one_axis(GY * 8)
    eye16, eye32 = np.eye(16), np.eye(32)
    ky = np.zeros((GY, 384, 256))
    kv = np.zeros((GY, 512, 256))
    for g in range(GY):
        for t in range(3):
            first = 8 * (g + t - 1)
            ky[g, t * 128 : t * 128 + 128, :128] = np.kron(eye16, window(once, first, 8, 8 * g, 8))
            ky[g, t * 128 : t * 128 + 128, 128:] = np.kron(eye16, window(twice, first, 8, 8 * g, 8))
        kv[g, :256] = np.kron(eye32, window(once, 8 * g, 8, 8 * g, 8))
        kv[g, 256:384] = np.kron(eye32, window(once, 8 * g - 4, 4, 8 * g, 8))
        kv[g, 384:] = np.kron(eye32, window(once, 8 * g + 8, 4, 8 * g, 8))
    return ky.astype(np.float32), kv.astype(np.float32)


def column_matrices():
    length = 128 * 3
    weights = one_axis(length)
    kx = np.zeros((3, 256, 256))
    for place, first in enumerate((0, 128, 256)):
        for k in range(2):
            rows = slice(k * 128, k * 128 + 128)
            kx[place, rows, :128] = window(weights[k], first, 128, first, 128).T
            kx[place, rows, 128:136] = window(weights[k], first - 8, 8, first, 128).T
            kx[place, rows, 136:144] = window(weights[k], first + 128, 8, first, 128).T
    return kx.astype(np.float32)


def split(matrix):
    hi = matrix.astype(BF16)
    return hi, (matrix - hi.astype(np.float32)).astype(BF16)


def stack(matrix, axis):
    hi, lo = split(matrix)
    return np.concatenate([hi, hi, lo], axis=axis)


def row_selection():
    top = np.kron(np.eye(32), np.eye(8)[:, :4])
    bottom = np.kron(np.eye(32), np.eye(8)[:, 4:])
    return np.concatenate([top, bottom], axis=1).astype(np.float32)


def mm(a, b):
    return jnp.dot(a, b, preferred_element_type=F32, precision=lax.Precision.HIGHEST)


def halves(x):
    hi = x.astype(BF16)
    return hi, (x - hi.astype(F32)).astype(BF16)


def times_matrix(x, stacked):
    hi, lo = halves(x)
    return jnp.dot(jnp.concatenate([hi, lo, hi], axis=1), stacked, preferred_element_type=F32)


def matrix_times(stacked, x):
    hi, lo = halves(x)
    parts = [hi, lo, hi]
    more = stacked.shape[1] - 3 * x.shape[0]
    if more:
        parts.append(jnp.zeros((more, x.shape[1]), BF16))
    return jnp.dot(stacked, jnp.concatenate(parts, axis=0), preferred_element_type=F32)


def table_rows(body):
    def four(c, carry):
        for k in range(4):
            body(pl.ds(c * 4 + k, 1), pl.ds(pl.multiple_of(c * 512 + k * 128, 128), 128))
        return carry

    lax.fori_loop(0, 8, four, 0)


def build_onehot(cell, onehot, t):
    index = lax.broadcasted_iota(jnp.int32, (256, 128), 0)

    def body(r, lanes):
        row = cell[t, r, :]
        key = ((row & 127) >> 6) * 128 + ((row >> 7) & 127)
        onehot[t, :, lanes] = jnp.where(index == key, 1.0, 0.0).astype(BF16)

    table_rows(body)


def pert_at_obs(pert, table, cell, onehot, got, po):
    for v in range(5):
        for m in range(2):
            block = pert[(m * 5 + v) * 128 : (m * 5 + v + 1) * 128, :].astype(F32).T.astype(BF16)
            for xq in range(2):
                table[(v * 2 + m) * 64 : (v * 2 + m + 1) * 64, xq * 128 : xq * 128 + 128] = block[xq * 64 : xq * 64 + 64]
    index = lax.broadcasted_iota(jnp.int32, (64, 128), 0)
    got[...] = jnp.dot(table[...], onehot[OWN], preferred_element_type=F32)

    def body(r, lanes):
        row = cell[OWN, r, :]
        key = (row >> 14) * 64 + (row & 63)
        for m in range(2):
            acc = jnp.zeros((64, 128), F32)
            for v in range(5):
                acc = jnp.where(index + 64 * v == key, got[(v * 2 + m) * 64 : (v * 2 + m + 1) * 64, lanes], acc)
            po[OWN, m, r, :] = jnp.sum(acc, axis=0, keepdims=True)

    table_rows(body)


def observe(field, left, cell, onehot, got, po, out):
    for m in range(2):
        for xq in range(2):
            hi, lo = halves(field[xq * 64 : xq * 64 + 64, m * 128 : m * 128 + 128])
            left[m * 128 : m * 128 + 64, xq * 128 : xq * 128 + 128] = hi
            left[m * 128 + 64 : m * 128 + 128, xq * 128 : xq * 128 + 128] = lo
    index = lax.broadcasted_iota(jnp.int32, (64, 128), 0)
    got[0:256, :] = jnp.dot(left[...], onehot[OWN], preferred_element_type=F32)

    def body(r, lanes):
        total = po[OWN, 0, r, :] * (got[0:64, lanes] + got[64:128, lanes])
        total += po[OWN, 1, r, :] * (got[128:192, lanes] + got[192:256, lanes])
        total = jnp.where(index == (cell[OWN, r, :] & 63), total, 0.0)
        out[r, :] = jnp.sum(total, axis=0, keepdims=True)

    table_rows(body)


def spread(t, q, cell, onehot, po, values, w):
    index = lax.broadcasted_iota(jnp.int32, (64, 128), 0)

    def body(r, lanes):
        mine = index == (cell[t, r, :] & 63)
        for m in range(2):
            value = po[t, m, r, :] * q[r, :]
            hi = value.astype(BF16).astype(F32)
            values[m * 128 : m * 128 + 64, lanes] = jnp.where(mine, hi, 0.0).astype(BF16)
            values[m * 128 + 64 : m * 128 + 128, lanes] = jnp.where(mine, value - hi, 0.0).astype(BF16)

    table_rows(body)
    got = lax.dot_general(values[...], onehot[t], (((1,), (1,)), ((), ())), preferred_element_type=F32)
    for m in range(2):
        for xq in range(2):
            lanes = slice(xq * 128, xq * 128 + 128)
            w[m * 128 + xq * 64 : m * 128 + xq * 64 + 64, t * 128 : t * 128 + 128] = (
                got[m * 128 : m * 128 + 64, lanes] + got[m * 128 + 64 : m * 128 + 128, lanes]
            )


def member_part(field, pert, out):
    turned = [field[:, m * 128 : m * 128 + 128].T for m in range(2)]
    for v in range(5):
        block = sum(pert[(m * 5 + v) * 128 : (m * 5 + v + 1) * 128, :].astype(F32) * turned[m] for m in range(2))
        for j in range(MEM):
            out[j, v] = block[j * 16 : j * 16 + 16]


def kernel(
    pert_in, ctrl_in, back_in, cell_in, flag_in, innov_in, prec_in, ky_in, kvo_in, kvh_in, kxo_in, kxs_in, sel_in,
    inc_out, state_out,
    pert, ctrl, back, cell, flag, innov, prec, ky, kvo, kvh, kxo, kxs, sel,
    onehot, table, left, values, got, po, q, w, exch, part, edges, fields,
    v_pack, v_edge, v_rows, v_strip, h_send, h_recv, w_send, w_recv, g_send, g_recv, r_send, r_recv,
    local_sem, send_sem, recv_sem, far_sem,
):
    me_m, me_y, me_x = lax.axis_index("mem"), lax.axis_index("gy"), lax.axis_index("gx")
    up, dn = {"gy": lax.rem(me_y + 3, GY)}, {"gy": lax.rem(me_y + 1, GY)}
    lf, rt = {"gx": lax.rem(me_x + 15, GX)}, {"gx": lax.rem(me_x + 1, GX)}

    def member_peer(i):
        return {"mem": lax.rem(me_m + i, MEM)}

    def tile_peer(i):
        return {
            "gy": lax.rem(me_y + lax.rem(i // GX + 1, GY), GY),
            "gx": lax.rem(me_x + lax.rem(lax.rem(i, GX) + 1, GX), GX),
        }

    place = jnp.where(me_x == 0, 0, jnp.where(me_x == GX - 1, 2, 1))
    loads = [
        (ctrl_in, ctrl),
        (sel_in, sel),
        (cell_in, cell.at[OWN]),
        (pert_in, pert),
        (kvo_in.at[me_y], kvo),
        (kvh_in.at[me_y], kvh),
        (kxo_in.at[place], kxo),
        (kxs_in.at[place], kxs),
        (flag_in, flag.at[OWN]),
        (innov_in, innov.at[OWN]),
        (prec_in, prec.at[OWN]),
        (ky_in.at[me_y], ky),
        (back_in, back),
    ]
    loads = [pltpu.make_async_copy(src, dst, local_sem.at[i]) for i, (src, dst) in enumerate(loads)]
    for load in loads:
        load.start()

    barrier = pltpu.get_barrier_semaphore()
    for device in (up, dn, lf, rt, {**up, **lf}, {**up, **rt}, {**dn, **lf}, {**dn, **rt}):
        pl.semaphore_signal(barrier, inc=1, device_id=device, device_id_type=MESH)
    for i in range(1, MEM):
        pl.semaphore_signal(barrier, inc=1, device_id=member_peer(i), device_id_type=MESH)

    sent, sent_all = [], []
    used = [0]

    def copy(src, dst, device):
        i = used[0]
        used[0] += 1
        out = pltpu.make_async_remote_copy(
            src_ref=src, dst_ref=dst, send_sem=send_sem.at[i], recv_sem=recv_sem.at[i], device_id=device, device_id_type=MESH
        )
        out.start()
        sent.append(out)
        return out

    def up_and_dn(ref):
        return [copy(ref.at[OWN], ref.at[DN], up), copy(ref.at[OWN], ref.at[UP], dn)]

    def to_members(source, into):
        base = used[0]
        used[0] += 1
        for i in range(1, MEM):
            pltpu.make_async_remote_copy(
                src_ref=source(i),
                dst_ref=into.at[i - 1],
                send_sem=send_sem.at[base],
                recv_sem=recv_sem.at[base],
                device_id=member_peer(i),
                device_id_type=MESH,
            ).start()
        sent_all.append((into, base))
        return pltpu.make_async_copy(into, into, recv_sem.at[base])

    loads[0].wait()
    field = jnp.concatenate([ctrl[0:128, :].T, ctrl[128:256, :].T], axis=1)
    loads[1].wait()
    packed = mm(field, sel[...])
    v_pack[0], v_pack[1] = packed[:, :128], packed[:, 128:]
    for m in range(2):
        v_edge[0, m] = field[0:8, m * 128 : m * 128 + 128]
        v_edge[1, m] = field[120:128, m * 128 : m * 128 + 128]
    loads[2].wait()

    pl.semaphore_wait(barrier, 8 + MEM - 1)

    first, last = pl.ds(0, 8), pl.ds(120, 8)
    halo = [
        copy(v_pack.at[0], v_rows.at[1], up),
        copy(v_pack.at[1], v_rows.at[0], dn),
        copy(v_pack.at[0, first], v_strip.at[RT, 3], {**up, **lf}),
        copy(v_pack.at[0, last], v_strip.at[LF, 3], {**up, **rt}),
        copy(v_pack.at[1, first], v_strip.at[RT, 2], {**dn, **lf}),
        copy(v_pack.at[1, last], v_strip.at[LF, 2], {**dn, **rt}),
        copy(v_edge.at[0], v_strip.at[RT, pl.ds(0, 2)], lf),
        copy(v_edge.at[1], v_strip.at[LF, pl.ds(0, 2)], rt),
    ]
    tables = up_and_dn(cell)

    build_onehot(cell, onehot, OWN)
    loads[3].wait()
    pert_at_obs(pert, table, cell, onehot, got, po)
    tables += up_and_dn(po)

    for load in loads[4:]:
        load.wait()
    rows_v = times_matrix(field, kvo[...])
    for one in halo:
        one.wait_recv()
    for offset in (2, GX - 2):
        pl.semaphore_signal(far_sem.at[0], inc=1, device_id={"gx": lax.rem(me_x + offset, GX)}, device_id_type=MESH)
    for ref in (innov, prec, flag):
        tables += up_and_dn(ref)
    rows_v += times_matrix(jnp.concatenate([v_rows[0], v_rows[1]], axis=1), kvh[...])
    near = [jnp.concatenate([v_strip[side, 0], v_strip[side, 1]], axis=1) for side in (LF, RT)]
    far = [jnp.concatenate([v_strip[side, 2], v_strip[side, 3]], axis=1) for side in (LF, RT)]
    strips = times_matrix(jnp.concatenate(near, axis=0), kvo[...]) + times_matrix(jnp.concatenate(far, axis=0), kvh[...])
    smoothed = matrix_times(kxo[0:128, :], rows_v) + matrix_times(kxs[0:128, :], strips)

    def members_total(phase):
        out = h_send[phase]
        for i in range(MEM - 1):
            out += h_recv[phase, i]
        return out

    def levels_total(k):
        out = r_send[k, me_m]
        for i in range(MEM - 1):
            out += r_recv[k, i]
        return out

    observe(smoothed, left, cell, onehot, got, po, h_send.at[0])
    h_send[0, 32:40, :] = jnp.zeros((8, 128), F32)
    arrived = to_members(lambda i: h_send.at[0], h_recv.at[0])
    for one in tables[0:2]:
        one.wait_recv()
    build_onehot(cell, onehot, UP)
    build_onehot(cell, onehot, DN)
    arrived.wait()
    exch[0, OWN] = members_total(0)[0:32]
    around = up_and_dn(exch.at[0])
    pl.semaphore_wait(far_sem.at[0], 2)
    for offset in (4, GX - 4):
        pl.semaphore_signal(far_sem.at[1], inc=1, device_id={"gx": lax.rem(me_x + offset, GX)}, device_id_type=MESH)
    state = field
    lane = lax.broadcasted_iota(jnp.int32, (1, 128), 1)
    levels = []

    def terms(t, seen):
        misfit = seen - innov[t]
        weight = jnp.where(flag[t] == 1, 1.0 / jnp.sqrt(1.0 + misfit * misfit), 1.0)
        inverse = prec[t] * weight
        q[t] = inverse * misfit
        return inverse

    def x_stage(along, rows):
        return [
            jnp.concatenate([along[0:rows, k * 128 : k * 128 + 128], along[rows : 2 * rows, k * 128 : k * 128 + 128]], axis=1)
            for k in range(2)
        ]

    for it in range(ITERS):
        for t in (OWN, UP, DN):
            if it == 0:
                if t == UP:
                    for one in tables[2:]:
                        one.wait_recv()
                    around[1].wait_recv()
                elif t == DN:
                    around[0].wait_recv()
                seen = exch[0, t]
            else:
                seen = exch[0, t] - step * exch[1, t]
            inverse_t = terms(t, seen)
            if t == OWN:
                inverse = inverse_t
            spread(t, q.at[t], cell, onehot, po, values, w)
        for m in range(2):
            w_send[it, 0, m * 8 : m * 8 + 8, :] = w[m * 128 : m * 128 + 8, :]
            w_send[it, 1, m * 8 : m * 8 + 8, :] = w[m * 128 + 120 : m * 128 + 128, :]
        sides = [copy(w_send.at[it, 0], w_recv.at[it, RT], lf), copy(w_send.at[it, 1], w_recv.at[it, LF], rt)]
        if it == ITERS - 1:
            member_part(smoothed, pert, r_send.at[0])
            levels.append(to_members(lambda i: r_send.at[0, lax.rem(me_m + i, MEM)], r_recv.at[0]))
        once, twice = x_stage(times_matrix(w[...], ky[...]), 128)
        part[0] = matrix_times(kxo[0:128, :], once)
        part[1] = matrix_times(kxo[128:256, :], twice)
        for one in sides:
            one.wait_recv()
        edge = [w_recv[it, side, m * 8 : m * 8 + 8, :] for m in range(2) for side in (LF, RT)]
        edges[...] = times_matrix(jnp.concatenate(edge, axis=0), ky[...])
        edge_once, edge_twice = x_stage(edges, 16)
        fields[it, 0] = matrix_times(kxs[0:128, :], edge_once)
        fields[it, 1] = matrix_times(kxs[128:256, :], edge_twice)
        grad = state + (part[0] + fields[it, 0])
        change = smoothed + (part[1] + fields[it, 1])
        observe(change, left, cell, onehot, got, po, h_send.at[it + 1])
        norm = jnp.sum((grad * grad).reshape(16, 8, 256), axis=0)
        h_send[it + 1, 32:40, :] = norm[:, 0:128] + norm[:, 128:256]
        arrived = to_members(lambda i: h_send.at[it + 1], h_recv.at[it + 1])
        if it == ITERS - 1:
            member_part(change, pert, r_send.at[1])
            levels.append(to_members(lambda i: r_send.at[1, lax.rem(me_m + i, MEM)], r_recv.at[1]))
        arrived.wait()
        totals = members_total(it + 1)
        delta = totals[0:32]
        norm = jnp.sum(totals[32:40], axis=0, keepdims=True)
        curv = jnp.sum(inverse * delta * delta, axis=0, keepdims=True)
        norm = norm + pltpu.roll(norm, 64, 1)
        curv = curv + pltpu.roll(curv, 64, 1)
        both = jnp.where(lane < 64, norm, curv)
        g_send[it] = both
        if it == 0:
            pl.semaphore_wait(far_sem.at[1], 2)
        base = used[0]
        used[0] += 1

        def to_tiles(i, carry):
            pltpu.make_async_remote_copy(
                src_ref=g_send.at[it],
                dst_ref=g_recv.at[it, i],
                send_sem=send_sem.at[base],
                recv_sem=recv_sem.at[base],
                device_id=tile_peer(i),
                device_id_type=MESH,
            ).start()
            return carry

        lax.fori_loop(0, TILES - 1, to_tiles, 0)
        sent_all.append((g_recv.at[it], base))
        if it < ITERS - 1:
            exch[it + 1, OWN] = delta
            around = up_and_dn(exch.at[it + 1])
            for one in around:
                one.wait_recv()
        else:
            for one in levels:
                one.wait()
            total_before, total_change = back[...] + levels_total(0), levels_total(1)
        pltpu.make_async_copy(g_recv.at[it], g_recv.at[it], recv_sem.at[base]).wait()
        both = both + jnp.sum(g_recv[it], axis=0)
        norm = jnp.sum(jnp.where(lane < 64, both, 0.0), axis=1, keepdims=True)
        curv = jnp.sum(jnp.where(lane < 64, 0.0, both), axis=1, keepdims=True)
        step = norm / (norm + curv)
        state = state - step * grad
        if it < ITERS - 1:
            smoothed = smoothed - step * change
    inc_out[...] = total_before - step.reshape(1, 1, 1) * total_change
    for m in range(2):
        state_out[m * 128 : m * 128 + 128, :] = state[:, m * 128 : m * 128 + 128].T
    for one in sent:
        one.wait_send()
    for ref, i in sent_all:
        pltpu.make_async_copy(ref, ref, send_sem.at[i]).wait()


def per_device(perturbations, control, background, obs_cell, huber_flag, innovation, precision):
    ky, kv = row_matrices()
    kx, sel = column_matrices(), row_selection()
    kxs = np.zeros((3, 256, 128), BF16)
    kxs[:, :, 0:48] = stack(kx[:, :, 128:144], 2)
    args = (
        perturbations.reshape(1280, 128), control.reshape(256, 128), background.reshape(5, 16, 128),
        obs_cell, huber_flag, innovation, precision,
        jnp.asarray(stack(ky, 1)), jnp.asarray(stack(kv[:, :256], 1)), jnp.asarray(stack(kv[:, 256:], 1)),
        jnp.asarray(stack(kx[:, :, :128], 2)), jnp.asarray(kxs), jnp.asarray(sel),
    )
    i32 = jnp.int32
    inc, state = pl.pallas_call(
        kernel,
        out_shape=(jax.ShapeDtypeStruct((5, 16, 128), F32), jax.ShapeDtypeStruct((256, 128), F32)),
        in_specs=[pl.BlockSpec(memory_space=pl.ANY)] * len(args),
        out_specs=(pl.BlockSpec(memory_space=pltpu.VMEM),) * 2,
        scratch_shapes=[
            pltpu.VMEM((1280, 128), BF16),
            pltpu.VMEM((256, 128), F32),
            pltpu.VMEM((5, 16, 128), F32),
            pltpu.VMEM((3, 32, 128), i32),
            pltpu.VMEM((3, 32, 128), i32),
            pltpu.VMEM((3, 32, 128), F32),
            pltpu.VMEM((3, 32, 128), F32),
            pltpu.VMEM((1152, 256), BF16),
            pltpu.VMEM((768, 256), BF16),
            pltpu.VMEM((768, 256), BF16),
            pltpu.VMEM((256, 384), BF16),
            pltpu.VMEM((256, 128), BF16),
            pltpu.VMEM((256, 256), F32),
            pltpu.VMEM((3, 256, 4096), BF16),
            pltpu.VMEM((640, 256), BF16),
            pltpu.VMEM((256, 256), BF16),
            pltpu.VMEM((256, 4096), BF16),
            pltpu.VMEM((640, 4096), F32),
            pltpu.VMEM((3, 2, 32, 128), F32),
            pltpu.VMEM((3, 32, 128), F32),
            pltpu.VMEM((256, 384), F32),
            pltpu.VMEM((ITERS, 3, 32, 128), F32),
            pltpu.VMEM((2, 128, 256), F32),
            pltpu.VMEM((32, 256), F32),
            pltpu.VMEM((ITERS, 2, 128, 256), F32),
            pltpu.VMEM((2, 128, 128), F32),
            pltpu.VMEM((2, 2, 8, 128), F32),
            pltpu.VMEM((2, 128, 128), F32),
            pltpu.VMEM((2, 4, 8, 128), F32),
            pltpu.VMEM((ITERS + 1, 40, 128), F32),
            pltpu.VMEM((ITERS + 1, MEM - 1, 40, 128), F32),
            pltpu.VMEM((ITERS, 2, 16, 384), F32),
            pltpu.VMEM((ITERS, 2, 16, 384), F32),
            pltpu.VMEM((ITERS, 1, 128), F32),
            pltpu.VMEM((ITERS, TILES - 1, 1, 128), F32),
            pltpu.VMEM((2, MEM, 5, 16, 128), F32),
            pltpu.VMEM((2, MEM - 1, 5, 16, 128), F32),
            pltpu.SemaphoreType.DMA((13,)),
            pltpu.SemaphoreType.DMA((40,)),
            pltpu.SemaphoreType.DMA((40,)),
            pltpu.SemaphoreType.REGULAR((2,)),
        ],
        compiler_params=pltpu.CompilerParams(collective_id=0, has_side_effects=True, vmem_limit_bytes=63 * 2**20 + 2**19),
    )(*args)
    return inc.reshape(background.shape), state.reshape(control.shape)


def solution(mesh):
    grid = P("mem", None, "gy", "gx")
    table = P("gy", "gx")
    return jax.shard_map(
        per_device,
        mesh=mesh,
        in_specs=(P("mem", None, None, "gy", "gx"), grid, P(None, "mem", "gy", "gx"), table, table, table, table),
        out_specs=(P(None, "mem", "gy", "gx"), grid),
        check_vma=False,
    )
```

```python
import functools

import jax
import jax.numpy as jnp
import numpy as np
from jax import lax
from jax.experimental import pallas as pl
from jax.experimental.pallas import tpu as pltpu
from jax.sharding import PartitionSpec as P

MESH = pl.DeviceIdType.MESH
F32, BF16 = jnp.float32, jnp.bfloat16
MEM, GY, GX = 8, 4, 16
TILES = GY * GX
ITERS = 2
FAR_FIRST = sorted(
    ((rows, cols) for rows in range(GY) for cols in range(GX) if rows or cols),
    key=lambda at: -(4 * min(at[0], GY - at[0]) + min(at[1], GX - at[1]) / 4),
)
UP, OWN, DN = 0, 1, 2
LF, RT = 0, 1


def taps():
    offsets = np.arange(-4, 5).astype(np.float32)
    raw = np.exp(-offsets * offsets / np.float32(8.0))
    return (raw / raw.sum()).astype(np.float64)


def one_axis(length):
    weights = taps()
    distance = np.arange(length)[None, :] - np.arange(length)[:, None]
    inside = np.abs(distance) <= 4
    once = np.where(inside, weights[np.clip(distance + 4, 0, 8)], 0.0)
    return once, once @ once


def window(full, first_in, rows, first_out, cols):
    out = np.zeros((rows, cols))
    for i in range(rows):
        if 0 <= first_in + i < full.shape[0]:
            out[i] = full[first_in + i, first_out : first_out + cols]
    return out


def row_matrices():
    once, twice = one_axis(GY * 8)
    eye16, eye32 = np.eye(16), np.eye(32)
    ky = np.zeros((GY, 384, 256))
    kv = np.zeros((GY, 512, 256))
    for g in range(GY):
        for t in range(3):
            first = 8 * (g + t - 1)
            ky[g, t * 128 : t * 128 + 128, :128] = np.kron(eye16, window(once, first, 8, 8 * g, 8))
            ky[g, t * 128 : t * 128 + 128, 128:] = np.kron(eye16, window(twice, first, 8, 8 * g, 8))
        kv[g, :256] = np.kron(eye32, window(once, 8 * g, 8, 8 * g, 8))
        kv[g, 256:384] = np.kron(eye32, window(once, 8 * g - 4, 4, 8 * g, 8))
        kv[g, 384:] = np.kron(eye32, window(once, 8 * g + 8, 4, 8 * g, 8))
    return ky.astype(np.float32), kv.astype(np.float32)


def column_matrices():
    length = 128 * 3
    weights = one_axis(length)
    kx = np.zeros((3, 256, 256))
    for place, first in enumerate((0, 128, 256)):
        for k in range(2):
            rows = slice(k * 128, k * 128 + 128)
            kx[place, rows, :128] = window(weights[k], first, 128, first, 128).T
            kx[place, rows, 128:136] = window(weights[k], first - 8, 8, first, 128).T
            kx[place, rows, 136:144] = window(weights[k], first + 128, 8, first, 128).T
    return kx.astype(np.float32)


def split(matrix):
    hi = matrix.astype(BF16)
    return hi, (matrix - hi.astype(np.float32)).astype(BF16)


def stack(matrix, axis):
    hi, lo = split(matrix)
    return np.concatenate([hi, hi, lo], axis=axis)


def row_selection():
    top = np.kron(np.eye(32), np.eye(8)[:, :4])
    bottom = np.kron(np.eye(32), np.eye(8)[:, 4:])
    return np.concatenate([top, bottom], axis=1).astype(np.float32)


def mm(a, b):
    return jnp.dot(a, b, preferred_element_type=F32, precision=lax.Precision.HIGHEST)


def halves(x):
    hi = x.astype(BF16)
    return hi, (x - hi.astype(F32)).astype(BF16)


def times_matrix(x, stacked):
    hi, lo = halves(x)
    return jnp.dot(jnp.concatenate([hi, lo, hi], axis=1), stacked, preferred_element_type=F32)


def matrix_times(stacked, x):
    hi, lo = halves(x)
    parts = [hi, lo, hi]
    more = stacked.shape[1] - 3 * x.shape[0]
    if more:
        parts.append(jnp.zeros((more, x.shape[1]), BF16))
    return jnp.dot(stacked, jnp.concatenate(parts, axis=0), preferred_element_type=F32)


def table_rows(body, first=0, last=8):
    def four(c, carry):
        for k in range(4):
            body(pl.ds(c * 4 + k, 1), pl.ds(pl.multiple_of(c * 512 + k * 128, 128), 128))
        return carry

    lax.fori_loop(first, last, four, 0)


def build_onehot(cell, onehot, t):
    index = lax.broadcasted_iota(jnp.int32, (256, 128), 0)

    def body(r, lanes):
        row = cell[t, r, :]
        key = ((row & 127) >> 6) * 128 + ((row >> 7) & 127)
        onehot[t, :, lanes] = jnp.where(index == key, 1.0, 0.0).astype(BF16)

    table_rows(body)


def pert_at_obs(pert, table, cell, onehot, got, po):
    for v in range(5):
        for m in range(2):
            block = pert[(m * 5 + v) * 128 : (m * 5 + v + 1) * 128, :].astype(F32).T.astype(BF16)
            for xq in range(2):
                table[(v * 2 + m) * 64 : (v * 2 + m + 1) * 64, xq * 128 : xq * 128 + 128] = block[xq * 64 : xq * 64 + 64]
    index = lax.broadcasted_iota(jnp.int32, (64, 128), 0)
    got[...] = jnp.dot(table[...], onehot[OWN], preferred_element_type=F32)

    def body(r, lanes):
        row = cell[OWN, r, :]
        key = (row >> 14) * 64 + (row & 63)
        for m in range(2):
            acc = jnp.zeros((64, 128), F32)
            for v in range(5):
                acc = jnp.where(index + 64 * v == key, got[(v * 2 + m) * 64 : (v * 2 + m + 1) * 64, lanes], acc)
            po[OWN, m, r, :] = jnp.sum(acc, axis=0, keepdims=True)

    table_rows(body)


def observe(field, left, cell, onehot, got, po, out):
    for m in range(2):
        for xq in range(2):
            hi, lo = halves(field[xq * 64 : xq * 64 + 64, m * 128 : m * 128 + 128])
            left[m * 128 : m * 128 + 64, xq * 128 : xq * 128 + 128] = hi
            left[m * 128 + 64 : m * 128 + 128, xq * 128 : xq * 128 + 128] = lo
    index = lax.broadcasted_iota(jnp.int32, (64, 128), 0)
    got[0:256, :] = jnp.dot(left[...], onehot[OWN], preferred_element_type=F32)

    def body(r, lanes):
        total = po[OWN, 0, r, :] * (got[0:64, lanes] + got[64:128, lanes])
        total += po[OWN, 1, r, :] * (got[128:192, lanes] + got[192:256, lanes])
        total = jnp.where(index == (cell[OWN, r, :] & 63), total, 0.0)
        out[r, :] = jnp.sum(total, axis=0, keepdims=True)

    return body


def spread(t, q, cell, onehot, po, values, w):
    index = lax.broadcasted_iota(jnp.int32, (64, 128), 0)

    def body(r, lanes):
        mine = index == (cell[t, r, :] & 63)
        for m in range(2):
            value = po[t, m, r, :] * q[r, :]
            hi = value.astype(BF16).astype(F32)
            values[m * 128 : m * 128 + 64, lanes] = jnp.where(mine, hi, 0.0).astype(BF16)
            values[m * 128 + 64 : m * 128 + 128, lanes] = jnp.where(mine, value - hi, 0.0).astype(BF16)

    table_rows(body)
    got = lax.dot_general(values[...], onehot[t], (((1,), (1,)), ((), ())), preferred_element_type=F32)
    for m in range(2):
        for xq in range(2):
            lanes = slice(xq * 128, xq * 128 + 128)
            w[m * 128 + xq * 64 : m * 128 + xq * 64 + 64, t * 128 : t * 128 + 128] = (
                got[m * 128 : m * 128 + 64, lanes] + got[m * 128 + 64 : m * 128 + 128, lanes]
            )


def spread_edges(t, q, cell, onehot, po, values, edge):
    index = lax.broadcasted_iota(jnp.int32, (8, 128), 0)

    def body(r, lanes):
        column = cell[t, r, :] & 63
        for m in range(2):
            value = po[t, m, r, :] * q[r, :]
            hi = value.astype(BF16).astype(F32)
            for side in range(2):
                mine = index + 56 * side == column
                both = jnp.concatenate([jnp.where(mine, hi, 0.0), jnp.where(mine, value - hi, 0.0)], axis=0)
                values[side * 32 + m * 16 : side * 32 + m * 16 + 16, lanes] = both.astype(BF16)

    table_rows(body)
    got = lax.dot_general(values[...], onehot[t], (((1,), (1,)), ((), ())), preferred_element_type=F32)
    for side in range(2):
        for m in range(2):
            block = got[side * 32 + m * 16 : side * 32 + m * 16 + 16, side * 128 : side * 128 + 128]
            edge[side, m * 8 : m * 8 + 8, t * 128 : t * 128 + 128] = block[0:8] + block[8:16]


def member_part(field, pert, out):
    turned = [field[:, m * 128 : m * 128 + 128].T for m in range(2)]
    for v in range(5):
        block = sum(pert[(m * 5 + v) * 128 : (m * 5 + v + 1) * 128, :].astype(F32) * turned[m] for m in range(2))
        for j in range(MEM):
            out[j, v] = block[j * 16 : j * 16 + 16]


def kernel(
    pert_in, ctrl_in, back_in, cell_in, flag_in, innov_in, prec_in, ky_in, kvo_in, kvh_in, kxo_in, kxs_in, sel_in,
    inc_out, state_out,
    pert, ctrl, back, cell, flag, innov, prec, ky, kvo, kvh, kxo, kxs, sel,
    onehot, table, left, values, edge_values, got, po, q, w, exch, part, edges, fields,
    v_pack, v_edge, v_rows, v_strip, h_send, h_recv, h_recv_b, w_send, w_recv, g_send, g_recv, r_send, r_recv,
    local_sem, send_sem, recv_sem, far_sem,
):
    me_m, me_y, me_x = lax.axis_index("mem"), lax.axis_index("gy"), lax.axis_index("gx")
    up, dn = {"gy": lax.rem(me_y + 3, GY)}, {"gy": lax.rem(me_y + 1, GY)}
    lf, rt = {"gx": lax.rem(me_x + 15, GX)}, {"gx": lax.rem(me_x + 1, GX)}

    def member_peer(i):
        return {"mem": lax.rem(me_m + i, MEM)}

    place = jnp.where(me_x == 0, 0, jnp.where(me_x == GX - 1, 2, 1))
    loads = [
        (ctrl_in, ctrl),
        (sel_in, sel),
        (cell_in, cell.at[OWN]),
        (pert_in, pert),
        (kvo_in.at[me_y], kvo),
        (kvh_in.at[me_y], kvh),
        (kxo_in.at[place], kxo),
        (kxs_in.at[place], kxs),
        (flag_in, flag.at[OWN]),
        (innov_in, innov.at[OWN]),
        (prec_in, prec.at[OWN]),
        (ky_in.at[me_y], ky),
        (back_in, back),
    ]
    loads = [pltpu.make_async_copy(src, dst, local_sem.at[i]) for i, (src, dst) in enumerate(loads)]
    for load in loads:
        load.start()

    barrier = pltpu.get_barrier_semaphore()
    for device in (up, dn, lf, rt, {**up, **lf}, {**up, **rt}, {**dn, **lf}, {**dn, **rt}):
        pl.semaphore_signal(barrier, inc=1, device_id=device, device_id_type=MESH)
    for i in range(1, MEM):
        pl.semaphore_signal(barrier, inc=1, device_id=member_peer(i), device_id_type=MESH)

    sent, sent_all = [], []
    used = [0]

    def copy(src, dst, device):
        i = used[0]
        used[0] += 1
        out = pltpu.make_async_remote_copy(
            src_ref=src, dst_ref=dst, send_sem=send_sem.at[i], recv_sem=recv_sem.at[i], device_id=device, device_id_type=MESH
        )
        out.start()
        sent.append(out)
        return out

    def up_and_dn(ref):
        return [copy(ref.at[OWN], ref.at[DN], up), copy(ref.at[OWN], ref.at[UP], dn)]

    def to_members(source, into):
        base = used[0]
        used[0] += 1
        for i in range(1, MEM):
            pltpu.make_async_remote_copy(
                src_ref=source(i),
                dst_ref=into.at[i - 1],
                send_sem=send_sem.at[base],
                recv_sem=recv_sem.at[base],
                device_id=member_peer(i),
                device_id_type=MESH,
            ).start()
        sent_all.append((into, base))
        return pltpu.make_async_copy(into, into, recv_sem.at[base])

    loads[0].wait()
    field = jnp.concatenate([ctrl[0:128, :].T, ctrl[128:256, :].T], axis=1)
    loads[1].wait()
    packed = mm(field, sel[...])
    v_pack[0], v_pack[1] = packed[:, :128], packed[:, 128:]
    for m in range(2):
        v_edge[0, m] = field[0:8, m * 128 : m * 128 + 128]
        v_edge[1, m] = field[120:128, m * 128 : m * 128 + 128]
    loads[2].wait()

    pl.semaphore_wait(barrier, 8 + MEM - 1)

    first, last = pl.ds(0, 8), pl.ds(120, 8)
    halo = [
        copy(v_pack.at[0], v_rows.at[1], up),
        copy(v_pack.at[1], v_rows.at[0], dn),
        copy(v_pack.at[0, first], v_strip.at[RT, 3], {**up, **lf}),
        copy(v_pack.at[0, last], v_strip.at[LF, 3], {**up, **rt}),
        copy(v_pack.at[1, first], v_strip.at[RT, 2], {**dn, **lf}),
        copy(v_pack.at[1, last], v_strip.at[LF, 2], {**dn, **rt}),
        copy(v_edge.at[0], v_strip.at[RT, pl.ds(0, 2)], lf),
        copy(v_edge.at[1], v_strip.at[LF, pl.ds(0, 2)], rt),
    ]
    tables = up_and_dn(cell)

    build_onehot(cell, onehot, OWN)
    loads[3].wait()
    pert_at_obs(pert, table, cell, onehot, got, po)
    tables += up_and_dn(po)

    for load in loads[4:]:
        load.wait()
    rows_v = times_matrix(field, kvo[...])
    for one in halo:
        one.wait_recv()
    for offset in (2, GX - 2):
        pl.semaphore_signal(far_sem.at[0], inc=1, device_id={"gx": lax.rem(me_x + offset, GX)}, device_id_type=MESH)
    for ref in (innov, prec, flag):
        tables += up_and_dn(ref)
    rows_v += times_matrix(jnp.concatenate([v_rows[0], v_rows[1]], axis=1), kvh[...])
    near = [jnp.concatenate([v_strip[side, 0], v_strip[side, 1]], axis=1) for side in (LF, RT)]
    far = [jnp.concatenate([v_strip[side, 2], v_strip[side, 3]], axis=1) for side in (LF, RT)]
    strips = times_matrix(jnp.concatenate(near, axis=0), kvo[...]) + times_matrix(jnp.concatenate(far, axis=0), kvh[...])
    smoothed = matrix_times(kxo[0:128, :], rows_v) + matrix_times(kxs[0:128, :], strips)

    def sum_members(body, phase, norm):
        table_rows(body, 0, 4)
        first_half = to_members(lambda i: h_send.at[phase, pl.ds(0, 16)], h_recv.at[phase])
        h_send[phase, 32:40, :] = norm
        table_rows(body, 4, 8)
        second_half = to_members(lambda i: h_send.at[phase, pl.ds(16, 24)], h_recv_b.at[phase])

        def total():
            first_half.wait()
            one = h_send[phase, 0:16, :]
            for i in range(MEM - 1):
                one += h_recv[phase, i]
            second_half.wait()
            two = h_send[phase, 16:40, :]
            for i in range(MEM - 1):
                two += h_recv_b[phase, i]
            return jnp.concatenate([one, two[0:16]], axis=0), two[16:24]

        return total

    def levels_total(k):
        out = r_send[k, me_m]
        for i in range(MEM - 1):
            out += r_recv[k, i]
        return out

    total = sum_members(observe(smoothed, left, cell, onehot, got, po, h_send.at[0]), 0, jnp.zeros((8, 128), F32))
    for one in tables[0:2]:
        one.wait_recv()
    build_onehot(cell, onehot, UP)
    build_onehot(cell, onehot, DN)
    exch[0, OWN] = total()[0]
    around = up_and_dn(exch.at[0])
    pl.semaphore_wait(far_sem.at[0], 2)
    for offset in (4, GX - 4):
        pl.semaphore_signal(far_sem.at[1], inc=1, device_id={"gx": lax.rem(me_x + offset, GX)}, device_id_type=MESH)
    state = field
    lane = lax.broadcasted_iota(jnp.int32, (1, 128), 1)
    levels = []

    def terms(t, seen):
        misfit = seen - innov[t]
        weight = jnp.where(flag[t] == 1, 1.0 / jnp.sqrt(1.0 + misfit * misfit), 1.0)
        inverse = prec[t] * weight
        q[t] = inverse * misfit
        return inverse

    def x_stage(along, rows):
        return [
            jnp.concatenate([along[0:rows, k * 128 : k * 128 + 128], along[rows : 2 * rows, k * 128 : k * 128 + 128]], axis=1)
            for k in range(2)
        ]

    for it in range(ITERS):
        for t in (OWN, UP, DN):
            if it == 0:
                if t == UP:
                    for one in tables[2:]:
                        one.wait_recv()
                    around[1].wait_recv()
                elif t == DN:
                    around[0].wait_recv()
                seen = exch[0, t]
            else:
                seen = exch[0, t] - step * exch[1, t]
            inverse_t = terms(t, seen)
            if t == OWN:
                inverse = inverse_t
            spread_edges(t, q.at[t], cell, onehot, po, edge_values, w_send.at[it])
            if it == 0 and t == OWN:
                spread(t, q.at[t], cell, onehot, po, values, w)
        sides = [copy(w_send.at[it, 0], w_recv.at[it, RT], lf), copy(w_send.at[it, 1], w_recv.at[it, LF], rt)]
        if it == ITERS - 1:
            member_part(smoothed, pert, r_send.at[0])
            levels.append(to_members(lambda i: r_send.at[0, lax.rem(me_m + i, MEM)], r_recv.at[0]))
        for t in (OWN, UP, DN):
            if it > 0 or t != OWN:
                spread(t, q.at[t], cell, onehot, po, values, w)
        once, twice = x_stage(times_matrix(w[...], ky[...]), 128)
        part[0] = matrix_times(kxo[0:128, :], once)
        part[1] = matrix_times(kxo[128:256, :], twice)
        for one in sides:
            one.wait_recv()
        edge = [w_recv[it, side, m * 8 : m * 8 + 8, :] for m in range(2) for side in (LF, RT)]
        edges[...] = times_matrix(jnp.concatenate(edge, axis=0), ky[...])
        edge_once, edge_twice = x_stage(edges, 16)
        fields[it, 0] = matrix_times(kxs[0:128, :], edge_once)
        fields[it, 1] = matrix_times(kxs[128:256, :], edge_twice)
        grad = state + (part[0] + fields[it, 0])
        change = smoothed + (part[1] + fields[it, 1])
        body = observe(change, left, cell, onehot, got, po, h_send.at[it + 1])
        norm = jnp.sum((grad * grad).reshape(16, 8, 256), axis=0)
        total = sum_members(body, it + 1, norm[:, 0:128] + norm[:, 128:256])
        if it == ITERS - 1:
            member_part(change, pert, r_send.at[1])
            levels.append(to_members(lambda i: r_send.at[1, lax.rem(me_m + i, MEM)], r_recv.at[1]))
        delta, norm = total()
        norm = jnp.sum(norm, axis=0, keepdims=True)
        curv = jnp.sum(inverse * delta * delta, axis=0, keepdims=True)
        norm = norm + pltpu.roll(norm, 64, 1)
        curv = curv + pltpu.roll(curv, 64, 1)
        both = jnp.where(lane < 64, norm, curv)
        g_send[it] = both
        if it == 0:
            pl.semaphore_wait(far_sem.at[1], 2)
        base = used[0]
        used[0] += 1

        for i, (rows, cols) in enumerate(FAR_FIRST):
            pltpu.make_async_remote_copy(
                src_ref=g_send.at[it],
                dst_ref=g_recv.at[it, i],
                send_sem=send_sem.at[base],
                recv_sem=recv_sem.at[base],
                device_id={"gy": lax.rem(me_y + rows, GY), "gx": lax.rem(me_x + cols, GX)},
                device_id_type=MESH,
            ).start()
        sent_all.append((g_recv.at[it], base))
        if it < ITERS - 1:
            exch[it + 1, OWN] = delta
            around = up_and_dn(exch.at[it + 1])
            for one in around:
                one.wait_recv()
        else:
            for one in levels:
                one.wait()
            total_before, total_change = back[...] + levels_total(0), levels_total(1)
            turned = [[x[:, m * 128 : m * 128 + 128].T for m in range(2)] for x in (state, grad)]
        pltpu.make_async_copy(g_recv.at[it], g_recv.at[it], recv_sem.at[base]).wait()
        both = both + jnp.sum(g_recv[it], axis=0)
        norm = jnp.sum(jnp.where(lane < 64, both, 0.0), axis=1, keepdims=True)
        curv = jnp.sum(jnp.where(lane < 64, 0.0, both), axis=1, keepdims=True)
        step = norm / (norm + curv)
        if it < ITERS - 1:
            state = state - step * grad
            smoothed = smoothed - step * change
    inc_out[...] = total_before - step.reshape(1, 1, 1) * total_change
    for m in range(2):
        state_out[m * 128 : m * 128 + 128, :] = turned[0][m] - step * turned[1][m]
    for one in sent:
        one.wait_send()
    for ref, i in sent_all:
        pltpu.make_async_copy(ref, ref, send_sem.at[i]).wait()


def per_device(perturbations, control, background, obs_cell, huber_flag, innovation, precision):
    ky, kv = row_matrices()
    kx, sel = column_matrices(), row_selection()
    kxs = np.zeros((3, 256, 128), BF16)
    kxs[:, :, 0:48] = stack(kx[:, :, 128:144], 2)
    args = (
        perturbations.reshape(1280, 128), control.reshape(256, 128), background.reshape(5, 16, 128),
        obs_cell, huber_flag, innovation, precision,
        jnp.asarray(stack(ky, 1)), jnp.asarray(stack(kv[:, :256], 1)), jnp.asarray(stack(kv[:, 256:], 1)),
        jnp.asarray(stack(kx[:, :, :128], 2)), jnp.asarray(kxs), jnp.asarray(sel),
    )
    i32 = jnp.int32
    inc, state = pl.pallas_call(
        kernel,
        out_shape=(jax.ShapeDtypeStruct((5, 16, 128), F32), jax.ShapeDtypeStruct((256, 128), F32)),
        in_specs=[pl.BlockSpec(memory_space=pl.ANY)] * len(args),
        out_specs=(pl.BlockSpec(memory_space=pltpu.VMEM),) * 2,
        scratch_shapes=[
            pltpu.VMEM((1280, 128), BF16),
            pltpu.VMEM((256, 128), F32),
            pltpu.VMEM((5, 16, 128), F32),
            pltpu.VMEM((3, 32, 128), i32),
            pltpu.VMEM((3, 32, 128), i32),
            pltpu.VMEM((3, 32, 128), F32),
            pltpu.VMEM((3, 32, 128), F32),
            pltpu.VMEM((1152, 256), BF16),
            pltpu.VMEM((768, 256), BF16),
            pltpu.VMEM((768, 256), BF16),
            pltpu.VMEM((256, 384), BF16),
            pltpu.VMEM((256, 128), BF16),
            pltpu.VMEM((256, 256), F32),
            pltpu.VMEM((3, 256, 4096), BF16),
            pltpu.VMEM((640, 256), BF16),
            pltpu.VMEM((256, 256), BF16),
            pltpu.VMEM((256, 4096), BF16),
            pltpu.VMEM((64, 4096), BF16),
            pltpu.VMEM((640, 4096), F32),
            pltpu.VMEM((3, 2, 32, 128), F32),
            pltpu.VMEM((3, 32, 128), F32),
            pltpu.VMEM((256, 384), F32),
            pltpu.VMEM((ITERS, 3, 32, 128), F32),
            pltpu.VMEM((2, 128, 256), F32),
            pltpu.VMEM((32, 256), F32),
            pltpu.VMEM((ITERS, 2, 128, 256), F32),
            pltpu.VMEM((2, 128, 128), F32),
            pltpu.VMEM((2, 2, 8, 128), F32),
            pltpu.VMEM((2, 128, 128), F32),
            pltpu.VMEM((2, 4, 8, 128), F32),
            pltpu.VMEM((ITERS + 1, 40, 128), F32),
            pltpu.VMEM((ITERS + 1, MEM - 1, 16, 128), F32),
            pltpu.VMEM((ITERS + 1, MEM - 1, 24, 128), F32),
            pltpu.VMEM((ITERS, 2, 16, 384), F32),
            pltpu.VMEM((ITERS, 2, 16, 384), F32),
            pltpu.VMEM((ITERS, 1, 128), F32),
            pltpu.VMEM((ITERS, TILES - 1, 1, 128), F32),
            pltpu.VMEM((2, MEM, 5, 16, 128), F32),
            pltpu.VMEM((2, MEM - 1, 5, 16, 128), F32),
            pltpu.SemaphoreType.DMA((13,)),
            pltpu.SemaphoreType.DMA((40,)),
            pltpu.SemaphoreType.DMA((40,)),
            pltpu.SemaphoreType.REGULAR((2,)),
        ],
        compiler_params=pltpu.CompilerParams(collective_id=0, has_side_effects=True, vmem_limit_bytes=63 * 2**20 + 2**19),
    )(*args)
    return inc.reshape(background.shape), state.reshape(control.shape)


def solution(mesh):
    grid = P("mem", None, "gy", "gx")
    table = P("gy", "gx")
    return jax.shard_map(
        per_device,
        mesh=mesh,
        in_specs=(P("mem", None, None, "gy", "gx"), grid, P(None, "mem", "gy", "gx"), table, table, table, table),
        out_specs=(P(None, "mem", "gy", "gx"), grid),
        check_vma=False,
    )
```

```python
import functools

import jax
import jax.numpy as jnp
import numpy as np
from jax import lax
from jax.experimental import pallas as pl
from jax.experimental.pallas import tpu as pltpu
from jax.sharding import PartitionSpec as P

MESH = pl.DeviceIdType.MESH
F32, BF16 = jnp.float32, jnp.bfloat16
MEM, GY, GX = 8, 4, 16
TILES = GY * GX
ITERS = 2
FAR_FIRST = sorted(
    ((rows, cols) for rows in range(GY) for cols in range(GX) if rows or cols),
    key=lambda at: -(4 * min(at[0], GY - at[0]) + min(at[1], GX - at[1]) / 4),
)
UP, OWN, DN = 0, 1, 2
LF, RT = 0, 1


def taps():
    offsets = np.arange(-4, 5).astype(np.float32)
    raw = np.exp(-offsets * offsets / np.float32(8.0))
    return (raw / raw.sum()).astype(np.float64)


def one_axis(length):
    weights = taps()
    distance = np.arange(length)[None, :] - np.arange(length)[:, None]
    inside = np.abs(distance) <= 4
    once = np.where(inside, weights[np.clip(distance + 4, 0, 8)], 0.0)
    return once, once @ once


def window(full, first_in, rows, first_out, cols):
    out = np.zeros((rows, cols))
    for i in range(rows):
        if 0 <= first_in + i < full.shape[0]:
            out[i] = full[first_in + i, first_out : first_out + cols]
    return out


def row_matrices():
    once, twice = one_axis(GY * 8)
    eye16, eye32 = np.eye(16), np.eye(32)
    ky = np.zeros((GY, 384, 256))
    kv = np.zeros((GY, 512, 256))
    for g in range(GY):
        for t in range(3):
            first = 8 * (g + t - 1)
            ky[g, t * 128 : t * 128 + 128, :128] = np.kron(eye16, window(once, first, 8, 8 * g, 8))
            ky[g, t * 128 : t * 128 + 128, 128:] = np.kron(eye16, window(twice, first, 8, 8 * g, 8))
        kv[g, :256] = np.kron(eye32, window(once, 8 * g, 8, 8 * g, 8))
        kv[g, 256:384] = np.kron(eye32, window(once, 8 * g - 4, 4, 8 * g, 8))
        kv[g, 384:] = np.kron(eye32, window(once, 8 * g + 8, 4, 8 * g, 8))
    return ky.astype(np.float32), kv.astype(np.float32)


def column_matrices():
    length = 128 * 3
    weights = one_axis(length)
    kx = np.zeros((3, 256, 256))
    for place, first in enumerate((0, 128, 256)):
        for k in range(2):
            rows = slice(k * 128, k * 128 + 128)
            kx[place, rows, :128] = window(weights[k], first, 128, first, 128).T
            kx[place, rows, 128:136] = window(weights[k], first - 8, 8, first, 128).T
            kx[place, rows, 136:144] = window(weights[k], first + 128, 8, first, 128).T
    return kx.astype(np.float32)


def split(matrix):
    hi = matrix.astype(BF16)
    return hi, (matrix - hi.astype(np.float32)).astype(BF16)


def stack(matrix, axis):
    hi, lo = split(matrix)
    return np.concatenate([hi, hi, lo], axis=axis)


def row_selection():
    top = np.kron(np.eye(32), np.eye(8)[:, :4])
    bottom = np.kron(np.eye(32), np.eye(8)[:, 4:])
    return np.concatenate([top, bottom], axis=1).astype(np.float32)


def mm(a, b):
    return jnp.dot(a, b, preferred_element_type=F32, precision=lax.Precision.HIGHEST)


def halves(x):
    hi = x.astype(BF16)
    return hi, (x - hi.astype(F32)).astype(BF16)


def times_matrix(x, stacked):
    hi, lo = halves(x)
    return jnp.dot(jnp.concatenate([hi, lo, hi], axis=1), stacked, preferred_element_type=F32)


def matrix_times(stacked, x):
    hi, lo = halves(x)
    parts = [hi, lo, hi]
    more = stacked.shape[1] - 3 * x.shape[0]
    if more:
        parts.append(jnp.zeros((more, x.shape[1]), BF16))
    return jnp.dot(stacked, jnp.concatenate(parts, axis=0), preferred_element_type=F32)


def table_rows(body, first=0, last=8):
    def four(c, carry):
        for k in range(4):
            body(pl.ds(c * 4 + k, 1), pl.ds(pl.multiple_of(c * 512 + k * 128, 128), 128))
        return carry

    lax.fori_loop(first, last, four, 0)


def build_onehot(cell, onehot, t):
    index = lax.broadcasted_iota(jnp.int32, (256, 128), 0)

    def body(r, lanes):
        row = cell[t, r, :]
        key = ((row & 127) >> 6) * 128 + ((row >> 7) & 127)
        onehot[t, :, lanes] = jnp.where(index == key, 1.0, 0.0).astype(BF16)

    table_rows(body)


def pert_at_obs(pert, table, cell, onehot, got, po):
    for v in range(5):
        for m in range(2):
            block = pert[(m * 5 + v) * 128 : (m * 5 + v + 1) * 128, :].astype(F32).T.astype(BF16)
            for xq in range(2):
                table[(v * 2 + m) * 64 : (v * 2 + m + 1) * 64, xq * 128 : xq * 128 + 128] = block[xq * 64 : xq * 64 + 64]
    index = lax.broadcasted_iota(jnp.int32, (64, 128), 0)
    got[...] = jnp.dot(table[...], onehot[OWN], preferred_element_type=F32)

    def body(r, lanes):
        row = cell[OWN, r, :]
        key = (row >> 14) * 64 + (row & 63)
        for m in range(2):
            acc = jnp.zeros((64, 128), F32)
            for v in range(5):
                acc = jnp.where(index + 64 * v == key, got[(v * 2 + m) * 64 : (v * 2 + m + 1) * 64, lanes], acc)
            po[OWN, m, r, :] = jnp.sum(acc, axis=0, keepdims=True)

    table_rows(body)


def observe(field, left, cell, onehot, got, po, out):
    for m in range(2):
        for xq in range(2):
            hi, lo = halves(field[xq * 64 : xq * 64 + 64, m * 128 : m * 128 + 128])
            left[m * 128 : m * 128 + 64, xq * 128 : xq * 128 + 128] = hi
            left[m * 128 + 64 : m * 128 + 128, xq * 128 : xq * 128 + 128] = lo
    index = lax.broadcasted_iota(jnp.int32, (64, 128), 0)
    got[0:256, :] = jnp.dot(left[...], onehot[OWN], preferred_element_type=F32)

    def body(r, lanes):
        total = po[OWN, 0, r, :] * (got[0:64, lanes] + got[64:128, lanes])
        total += po[OWN, 1, r, :] * (got[128:192, lanes] + got[192:256, lanes])
        total = jnp.where(index == (cell[OWN, r, :] & 63), total, 0.0)
        out[r, :] = jnp.sum(total, axis=0, keepdims=True)

    return body


def spread(t, q, cell, onehot, po, values, w):
    index = lax.broadcasted_iota(jnp.int32, (64, 128), 0)

    def body(r, lanes):
        mine = index == (cell[t, r, :] & 63)
        for m in range(2):
            value = po[t, m, r, :] * q[r, :]
            hi = value.astype(BF16).astype(F32)
            values[m * 128 : m * 128 + 64, lanes] = jnp.where(mine, hi, 0.0).astype(BF16)
            values[m * 128 + 64 : m * 128 + 128, lanes] = jnp.where(mine, value - hi, 0.0).astype(BF16)

    table_rows(body)
    got = lax.dot_general(values[...], onehot[t], (((1,), (1,)), ((), ())), preferred_element_type=F32)
    for m in range(2):
        for xq in range(2):
            lanes = slice(xq * 128, xq * 128 + 128)
            w[m * 128 + xq * 64 : m * 128 + xq * 64 + 64, t * 128 : t * 128 + 128] = (
                got[m * 128 : m * 128 + 64, lanes] + got[m * 128 + 64 : m * 128 + 128, lanes]
            )


def spread_edges(t, q, cell, onehot, po, values, edge):
    index = lax.broadcasted_iota(jnp.int32, (8, 128), 0)

    def body(r, lanes):
        column = cell[t, r, :] & 63
        for m in range(2):
            value = po[t, m, r, :] * q[r, :]
            hi = value.astype(BF16).astype(F32)
            for side in range(2):
                mine = index + 56 * side == column
                both = jnp.concatenate([jnp.where(mine, hi, 0.0), jnp.where(mine, value - hi, 0.0)], axis=0)
                values[side * 32 + m * 16 : side * 32 + m * 16 + 16, lanes] = both.astype(BF16)

    table_rows(body)
    got = lax.dot_general(values[...], onehot[t], (((1,), (1,)), ((), ())), preferred_element_type=F32)
    for side in range(2):
        for m in range(2):
            block = got[side * 32 + m * 16 : side * 32 + m * 16 + 16, side * 128 : side * 128 + 128]
            edge[side, m * 8 : m * 8 + 8, t * 128 : t * 128 + 128] = block[0:8] + block[8:16]


def member_part(field, pert, out):
    turned = [field[:, m * 128 : m * 128 + 128].T for m in range(2)]
    for v in range(5):
        block = sum(pert[(m * 5 + v) * 128 : (m * 5 + v + 1) * 128, :].astype(F32) * turned[m] for m in range(2))
        for j in range(MEM):
            out[j, v] = block[j * 16 : j * 16 + 16]


def kernel(
    pert_in, ctrl_in, back_in, cell_in, flag_in, innov_in, prec_in, ky_in, kvo_in, kvh_in, kxo_in, kxs_in, sel_in,
    inc_out, state_out,
    pert, ctrl, back, cell, flag, innov, prec, ky, kvo, kvh, kxo, kxs, sel,
    onehot, table, left, values, edge_values, got, po, q, w, exch, part, edges, fields,
    v_pack, v_edge, v_rows, v_strip, h_send, h_recv, h_recv_b, w_send, w_recv, g_send, g_recv, r_send, r_recv,
    local_sem, send_sem, recv_sem, far_sem,
):
    me_m, me_y, me_x = lax.axis_index("mem"), lax.axis_index("gy"), lax.axis_index("gx")
    up, dn = {"gy": lax.rem(me_y + 3, GY)}, {"gy": lax.rem(me_y + 1, GY)}
    lf, rt = {"gx": lax.rem(me_x + 15, GX)}, {"gx": lax.rem(me_x + 1, GX)}

    def member_peer(i):
        return {"mem": lax.rem(me_m + i, MEM)}

    place = jnp.where(me_x == 0, 0, jnp.where(me_x == GX - 1, 2, 1))
    loads = [
        (ctrl_in, ctrl),
        (sel_in, sel),
        (cell_in, cell.at[OWN]),
        (pert_in, pert),
        (kvo_in.at[me_y], kvo),
        (kvh_in.at[me_y], kvh),
        (kxo_in.at[place], kxo),
        (kxs_in.at[place], kxs),
        (flag_in, flag.at[OWN]),
        (innov_in, innov.at[OWN]),
        (prec_in, prec.at[OWN]),
        (ky_in.at[me_y], ky),
        (back_in, back),
    ]
    loads = [pltpu.make_async_copy(src, dst, local_sem.at[i]) for i, (src, dst) in enumerate(loads)]
    for load in loads:
        load.start()

    barrier = pltpu.get_barrier_semaphore()
    for device in (up, dn, lf, rt, {**up, **lf}, {**up, **rt}, {**dn, **lf}, {**dn, **rt}):
        pl.semaphore_signal(barrier, inc=1, device_id=device, device_id_type=MESH)
    for i in range(1, MEM):
        pl.semaphore_signal(barrier, inc=1, device_id=member_peer(i), device_id_type=MESH)

    sent, sent_all = [], []
    used = [0]

    def copy(src, dst, device):
        i = used[0]
        used[0] += 1
        out = pltpu.make_async_remote_copy(
            src_ref=src, dst_ref=dst, send_sem=send_sem.at[i], recv_sem=recv_sem.at[i], device_id=device, device_id_type=MESH
        )
        out.start()
        sent.append(out)
        return out

    def up_and_dn(ref):
        return [copy(ref.at[OWN], ref.at[DN], up), copy(ref.at[OWN], ref.at[UP], dn)]

    def to_members(source, into):
        base = used[0]
        used[0] += 1
        for i in range(1, MEM):
            pltpu.make_async_remote_copy(
                src_ref=source(i),
                dst_ref=into.at[i - 1],
                send_sem=send_sem.at[base],
                recv_sem=recv_sem.at[base],
                device_id=member_peer(i),
                device_id_type=MESH,
            ).start()
        sent_all.append((into, base))
        return pltpu.make_async_copy(into, into, recv_sem.at[base])

    loads[0].wait()
    field = jnp.concatenate([ctrl[0:128, :].T, ctrl[128:256, :].T], axis=1)
    loads[1].wait()
    packed = mm(field, sel[...])
    v_pack[0], v_pack[1] = packed[:, :128], packed[:, 128:]
    for m in range(2):
        v_edge[0, m] = field[0:8, m * 128 : m * 128 + 128]
        v_edge[1, m] = field[120:128, m * 128 : m * 128 + 128]
    loads[2].wait()

    pl.semaphore_wait(barrier, 8 + MEM - 1)

    first, last = pl.ds(0, 8), pl.ds(120, 8)
    halo = [
        copy(v_pack.at[0], v_rows.at[1], up),
        copy(v_pack.at[1], v_rows.at[0], dn),
        copy(v_pack.at[0, first], v_strip.at[RT, 3], {**up, **lf}),
        copy(v_pack.at[0, last], v_strip.at[LF, 3], {**up, **rt}),
        copy(v_pack.at[1, first], v_strip.at[RT, 2], {**dn, **lf}),
        copy(v_pack.at[1, last], v_strip.at[LF, 2], {**dn, **rt}),
        copy(v_edge.at[0], v_strip.at[RT, pl.ds(0, 2)], lf),
        copy(v_edge.at[1], v_strip.at[LF, pl.ds(0, 2)], rt),
    ]
    tables = up_and_dn(cell)

    build_onehot(cell, onehot, OWN)
    loads[3].wait()
    pert_at_obs(pert, table, cell, onehot, got, po)
    tables += up_and_dn(po)

    for load in loads[4:]:
        load.wait()
    rows_v = times_matrix(field, kvo[...])
    for one in halo:
        one.wait_recv()
    for offset in (2, GX - 2):
        pl.semaphore_signal(far_sem.at[0], inc=1, device_id={"gx": lax.rem(me_x + offset, GX)}, device_id_type=MESH)
    for ref in (innov, prec, flag):
        tables += up_and_dn(ref)
    rows_v += times_matrix(jnp.concatenate([v_rows[0], v_rows[1]], axis=1), kvh[...])
    near = [jnp.concatenate([v_strip[side, 0], v_strip[side, 1]], axis=1) for side in (LF, RT)]
    far = [jnp.concatenate([v_strip[side, 2], v_strip[side, 3]], axis=1) for side in (LF, RT)]
    strips = times_matrix(jnp.concatenate(near, axis=0), kvo[...]) + times_matrix(jnp.concatenate(far, axis=0), kvh[...])
    smoothed = matrix_times(kxo[0:128, :], rows_v) + matrix_times(kxs[0:128, :], strips)

    def sum_members(body, phase, norm):
        table_rows(body, 0, 4)
        first_half = to_members(lambda i: h_send.at[phase, pl.ds(0, 16)], h_recv.at[phase])
        h_send[phase, 32:40, :] = norm
        table_rows(body, 4, 8)
        second_half = to_members(lambda i: h_send.at[phase, pl.ds(16, 24)], h_recv_b.at[phase])

        def total():
            first_half.wait()
            one = h_send[phase, 0:16, :]
            for i in range(MEM - 1):
                one += h_recv[phase, i]
            second_half.wait()
            two = h_send[phase, 16:40, :]
            for i in range(MEM - 1):
                two += h_recv_b[phase, i]
            return jnp.concatenate([one, two[0:16]], axis=0), two[16:24]

        return total

    def levels_total(k):
        out = r_send[k, me_m]
        for i in range(MEM - 1):
            out += r_recv[k, i]
        return out

    total = sum_members(observe(smoothed, left, cell, onehot, got, po, h_send.at[0]), 0, jnp.zeros((8, 128), F32))
    for one in tables[0:2]:
        one.wait_recv()
    build_onehot(cell, onehot, UP)
    build_onehot(cell, onehot, DN)
    exch[0, OWN] = total()[0]
    around = up_and_dn(exch.at[0])
    pl.semaphore_wait(far_sem.at[0], 2)
    for offset in (4, GX - 4):
        pl.semaphore_signal(far_sem.at[1], inc=1, device_id={"gx": lax.rem(me_x + offset, GX)}, device_id_type=MESH)
    state = field
    lane = lax.broadcasted_iota(jnp.int32, (1, 128), 1)
    levels = []

    def terms(t, seen):
        misfit = seen - innov[t]
        weight = jnp.where(flag[t] == 1, 1.0 / jnp.sqrt(1.0 + misfit * misfit), 1.0)
        inverse = prec[t] * weight
        q[t] = inverse * misfit
        return inverse

    def x_stage(along, rows):
        return [
            jnp.concatenate([along[0:rows, k * 128 : k * 128 + 128], along[rows : 2 * rows, k * 128 : k * 128 + 128]], axis=1)
            for k in range(2)
        ]

    for it in range(ITERS):
        for t in (OWN, UP, DN):
            if it == 0:
                if t == UP:
                    for one in tables[2:]:
                        one.wait_recv()
                    around[1].wait_recv()
                elif t == DN:
                    around[0].wait_recv()
                seen = exch[0, t]
            else:
                seen = exch[0, t] - step * exch[1, t]
            inverse_t = terms(t, seen)
            if t == OWN:
                inverse = inverse_t
            spread_edges(t, q.at[t], cell, onehot, po, edge_values, w_send.at[it])
            if it == 0 and t == OWN:
                spread(t, q.at[t], cell, onehot, po, values, w)
        sides = [copy(w_send.at[it, 0], w_recv.at[it, RT], lf), copy(w_send.at[it, 1], w_recv.at[it, LF], rt)]
        if it == ITERS - 1:
            member_part(smoothed, pert, r_send.at[0])
            levels.append(to_members(lambda i: r_send.at[0, lax.rem(me_m + i, MEM)], r_recv.at[0]))
        for t in (OWN, UP, DN):
            if it > 0 or t != OWN:
                spread(t, q.at[t], cell, onehot, po, values, w)
        once, twice = x_stage(times_matrix(w[...], ky[...]), 128)
        part[0] = matrix_times(kxo[0:128, :], once)
        part[1] = matrix_times(kxo[128:256, :], twice)
        for one in sides:
            one.wait_recv()
        edge = [w_recv[it, side, m * 8 : m * 8 + 8, :] for m in range(2) for side in (LF, RT)]
        edges[...] = times_matrix(jnp.concatenate(edge, axis=0), ky[...])
        edge_once, edge_twice = x_stage(edges, 16)
        fields[it, 0] = matrix_times(kxs[0:128, :], edge_once)
        fields[it, 1] = matrix_times(kxs[128:256, :], edge_twice)
        grad = state + (part[0] + fields[it, 0])
        change = smoothed + (part[1] + fields[it, 1])
        body = observe(change, left, cell, onehot, got, po, h_send.at[it + 1])
        norm = jnp.sum((grad * grad).reshape(16, 8, 256), axis=0)
        total = sum_members(body, it + 1, norm[:, 0:128] + norm[:, 128:256])
        if it == ITERS - 1:
            member_part(change, pert, r_send.at[1])
            levels.append(to_members(lambda i: r_send.at[1, lax.rem(me_m + i, MEM)], r_recv.at[1]))
        delta, norm = total()
        norm = jnp.sum(norm, axis=0, keepdims=True)
        curv = jnp.sum(inverse * delta * delta, axis=0, keepdims=True)
        norm = norm + pltpu.roll(norm, 64, 1)
        curv = curv + pltpu.roll(curv, 64, 1)
        both = jnp.where(lane < 64, norm, curv)
        g_send[it] = both
        if it == 0:
            pl.semaphore_wait(far_sem.at[1], 2)
        base = used[0]
        used[0] += 1

        for i, (rows, cols) in enumerate(FAR_FIRST):
            pltpu.make_async_remote_copy(
                src_ref=g_send.at[it],
                dst_ref=g_recv.at[it, i],
                send_sem=send_sem.at[base],
                recv_sem=recv_sem.at[base],
                device_id={"gy": lax.rem(me_y + rows, GY), "gx": lax.rem(me_x + cols, GX)},
                device_id_type=MESH,
            ).start()
        sent_all.append((g_recv.at[it], base))
        if it < ITERS - 1:
            exch[it + 1, OWN] = delta
            around = up_and_dn(exch.at[it + 1])
            for one in around:
                one.wait_recv()
        else:
            for one in levels:
                one.wait()
            total_before, total_change = back[...] + levels_total(0), levels_total(1)
            turned = [[x[:, m * 128 : m * 128 + 128].T for m in range(2)] for x in (state, grad)]
        pltpu.make_async_copy(g_recv.at[it], g_recv.at[it], recv_sem.at[base]).wait()
        both = both + jnp.sum(g_recv[it], axis=0)
        norm = jnp.sum(jnp.where(lane < 64, both, 0.0), axis=1, keepdims=True)
        curv = jnp.sum(jnp.where(lane < 64, 0.0, both), axis=1, keepdims=True)
        step = norm / (norm + curv)
        if it < ITERS - 1:
            state = state - step * grad
            smoothed = smoothed - step * change
    inc_out[...] = total_before - step.reshape(1, 1, 1) * total_change
    for m in range(2):
        state_out[m * 128 : m * 128 + 128, :] = turned[0][m] - step * turned[1][m]
    for one in sent:
        one.wait_send()
    for ref, i in sent_all:
        pltpu.make_async_copy(ref, ref, send_sem.at[i]).wait()


def deliver(inc_in, state_in, inc_out, state_out, sem):
    parts = [(inc_in, inc_out), (state_in.at[0:128], state_out.at[0:128]), (state_in.at[128:256], state_out.at[128:256])]
    copies = [pltpu.make_async_copy(src, dst, sem.at[i]) for i, (src, dst) in enumerate(parts)]
    for one in copies:
        one.start()
    for one in copies:
        one.wait()


def per_device(perturbations, control, background, obs_cell, huber_flag, innovation, precision):
    ky, kv = row_matrices()
    kx, sel = column_matrices(), row_selection()
    kxs = np.zeros((3, 256, 128), BF16)
    kxs[:, :, 0:48] = stack(kx[:, :, 128:144], 2)
    args = (
        perturbations.reshape(1280, 128), control.reshape(256, 128), background.reshape(5, 16, 128),
        obs_cell, huber_flag, innovation, precision,
        jnp.asarray(stack(ky, 1)), jnp.asarray(stack(kv[:, :256], 1)), jnp.asarray(stack(kv[:, 256:], 1)),
        jnp.asarray(stack(kx[:, :, :128], 2)), jnp.asarray(kxs), jnp.asarray(sel),
    )
    i32 = jnp.int32
    inc, state = pl.pallas_call(
        kernel,
        out_shape=(jax.ShapeDtypeStruct((5, 16, 128), F32), jax.ShapeDtypeStruct((256, 128), F32)),
        in_specs=[pl.BlockSpec(memory_space=pl.ANY)] * len(args),
        out_specs=(pl.BlockSpec(memory_space=pltpu.VMEM),) * 2,
        scratch_shapes=[
            pltpu.VMEM((1280, 128), BF16),
            pltpu.VMEM((256, 128), F32),
            pltpu.VMEM((5, 16, 128), F32),
            pltpu.VMEM((3, 32, 128), i32),
            pltpu.VMEM((3, 32, 128), i32),
            pltpu.VMEM((3, 32, 128), F32),
            pltpu.VMEM((3, 32, 128), F32),
            pltpu.VMEM((1152, 256), BF16),
            pltpu.VMEM((768, 256), BF16),
            pltpu.VMEM((768, 256), BF16),
            pltpu.VMEM((256, 384), BF16),
            pltpu.VMEM((256, 128), BF16),
            pltpu.VMEM((256, 256), F32),
            pltpu.VMEM((3, 256, 4096), BF16),
            pltpu.VMEM((640, 256), BF16),
            pltpu.VMEM((256, 256), BF16),
            pltpu.VMEM((256, 4096), BF16),
            pltpu.VMEM((64, 4096), BF16),
            pltpu.VMEM((640, 4096), F32),
            pltpu.VMEM((3, 2, 32, 128), F32),
            pltpu.VMEM((3, 32, 128), F32),
            pltpu.VMEM((256, 384), F32),
            pltpu.VMEM((ITERS, 3, 32, 128), F32),
            pltpu.VMEM((2, 128, 256), F32),
            pltpu.VMEM((32, 256), F32),
            pltpu.VMEM((ITERS, 2, 128, 256), F32),
            pltpu.VMEM((2, 128, 128), F32),
            pltpu.VMEM((2, 2, 8, 128), F32),
            pltpu.VMEM((2, 128, 128), F32),
            pltpu.VMEM((2, 4, 8, 128), F32),
            pltpu.VMEM((ITERS + 1, 40, 128), F32),
            pltpu.VMEM((ITERS + 1, MEM - 1, 16, 128), F32),
            pltpu.VMEM((ITERS + 1, MEM - 1, 24, 128), F32),
            pltpu.VMEM((ITERS, 2, 16, 384), F32),
            pltpu.VMEM((ITERS, 2, 16, 384), F32),
            pltpu.VMEM((ITERS, 1, 128), F32),
            pltpu.VMEM((ITERS, TILES - 1, 1, 128), F32),
            pltpu.VMEM((2, MEM, 5, 16, 128), F32),
            pltpu.VMEM((2, MEM - 1, 5, 16, 128), F32),
            pltpu.SemaphoreType.DMA((13,)),
            pltpu.SemaphoreType.DMA((40,)),
            pltpu.SemaphoreType.DMA((40,)),
            pltpu.SemaphoreType.REGULAR((2,)),
        ],
        compiler_params=pltpu.CompilerParams(collective_id=0, has_side_effects=True, vmem_limit_bytes=63 * 2**20 + 2**19),
    )(*args)
    inc, state = pl.pallas_call(
        deliver,
        out_shape=(jax.ShapeDtypeStruct(inc.shape, F32), jax.ShapeDtypeStruct(state.shape, F32)),
        in_specs=[pl.BlockSpec(memory_space=pl.ANY)] * 2,
        out_specs=(pl.BlockSpec(memory_space=pl.ANY),) * 2,
        scratch_shapes=[pltpu.SemaphoreType.DMA((3,))],
        compiler_params=pltpu.CompilerParams(vmem_limit_bytes=63 * 2**20 + 2**19),
    )(inc, state)
    return inc.reshape(background.shape), state.reshape(control.shape)


def solution(mesh):
    grid = P("mem", None, "gy", "gx")
    table = P("gy", "gx")
    return jax.shard_map(
        per_device,
        mesh=mesh,
        in_specs=(P("mem", None, None, "gy", "gx"), grid, P(None, "mem", "gy", "gx"), table, table, table, table),
        out_specs=(P(None, "mem", "gy", "gx"), grid),
        check_vma=False,
    )
```

```python
import functools

import jax
import jax.numpy as jnp
import numpy as np
from jax import lax
from jax.experimental import pallas as pl
from jax.experimental.pallas import tpu as pltpu
from jax.sharding import PartitionSpec as P

MESH = pl.DeviceIdType.MESH
F32, BF16 = jnp.float32, jnp.bfloat16
MEM, GY, GX = 8, 4, 16
TILES = GY * GX
ITERS = 2
FAR_FIRST = sorted(
    ((rows, cols) for rows in range(GY) for cols in range(GX) if rows or cols),
    key=lambda at: -(4 * min(at[0], GY - at[0]) + min(at[1], GX - at[1]) / 4),
)
UP, OWN, DN = 0, 1, 2
LF, RT = 0, 1


def taps():
    offsets = np.arange(-4, 5).astype(np.float32)
    raw = np.exp(-offsets * offsets / np.float32(8.0))
    return (raw / raw.sum()).astype(np.float64)


def one_axis(length):
    weights = taps()
    distance = np.arange(length)[None, :] - np.arange(length)[:, None]
    inside = np.abs(distance) <= 4
    once = np.where(inside, weights[np.clip(distance + 4, 0, 8)], 0.0)
    return once, once @ once


def window(full, first_in, rows, first_out, cols):
    out = np.zeros((rows, cols))
    for i in range(rows):
        if 0 <= first_in + i < full.shape[0]:
            out[i] = full[first_in + i, first_out : first_out + cols]
    return out


def row_matrices():
    once, twice = one_axis(GY * 8)
    eye16, eye32 = np.eye(16), np.eye(32)
    ky = np.zeros((GY, 384, 256))
    kv = np.zeros((GY, 512, 256))
    for g in range(GY):
        for t in range(3):
            first = 8 * (g + t - 1)
            ky[g, t * 128 : t * 128 + 128, :128] = np.kron(eye16, window(once, first, 8, 8 * g, 8))
            ky[g, t * 128 : t * 128 + 128, 128:] = np.kron(eye16, window(twice, first, 8, 8 * g, 8))
        kv[g, :256] = np.kron(eye32, window(once, 8 * g, 8, 8 * g, 8))
        kv[g, 256:384] = np.kron(eye32, window(once, 8 * g - 4, 4, 8 * g, 8))
        kv[g, 384:] = np.kron(eye32, window(once, 8 * g + 8, 4, 8 * g, 8))
    return ky.astype(np.float32), kv.astype(np.float32)


def column_matrices():
    length = 128 * 3
    weights = one_axis(length)
    kx = np.zeros((3, 256, 256))
    for place, first in enumerate((0, 128, 256)):
        for k in range(2):
            rows = slice(k * 128, k * 128 + 128)
            kx[place, rows, :128] = window(weights[k], first, 128, first, 128).T
            kx[place, rows, 128:136] = window(weights[k], first - 8, 8, first, 128).T
            kx[place, rows, 136:144] = window(weights[k], first + 128, 8, first, 128).T
    return kx.astype(np.float32)


def split(matrix):
    hi = matrix.astype(BF16)
    return hi, (matrix - hi.astype(np.float32)).astype(BF16)


def stack(matrix, axis):
    hi, lo = split(matrix)
    return np.concatenate([hi, hi, lo], axis=axis)


def row_selection():
    top = np.kron(np.eye(32), np.eye(8)[:, :4])
    bottom = np.kron(np.eye(32), np.eye(8)[:, 4:])
    return np.concatenate([top, bottom], axis=1).astype(np.float32)


def mm(a, b):
    return jnp.dot(a, b, preferred_element_type=F32, precision=lax.Precision.HIGHEST)


def halves(x):
    hi = x.astype(BF16)
    return hi, (x - hi.astype(F32)).astype(BF16)


def times_matrix(x, stacked):
    hi, lo = halves(x)
    return jnp.dot(jnp.concatenate([hi, lo, hi], axis=1), stacked, preferred_element_type=F32)


def matrix_times(stacked, x):
    hi, lo = halves(x)
    parts = [hi, lo, hi]
    more = stacked.shape[1] - 3 * x.shape[0]
    if more:
        parts.append(jnp.zeros((more, x.shape[1]), BF16))
    return jnp.dot(stacked, jnp.concatenate(parts, axis=0), preferred_element_type=F32)


def table_rows(body, first=0, last=8):
    def four(c, carry):
        for k in range(4):
            body(pl.ds(c * 4 + k, 1), pl.ds(pl.multiple_of(c * 512 + k * 128, 128), 128))
        return carry

    lax.fori_loop(first, last, four, 0)


def build_onehot(cell, onehot, t):
    index = lax.broadcasted_iota(jnp.int32, (256, 128), 0)

    def body(r, lanes):
        row = cell[t, r, :]
        key = ((row & 127) >> 6) * 128 + ((row >> 7) & 127)
        onehot[t, :, lanes] = jnp.where(index == key, 1.0, 0.0).astype(BF16)

    table_rows(body)


def pert_at_obs(pert, table, cell, onehot, got, po):
    for v in range(5):
        for m in range(2):
            block = pert[(m * 5 + v) * 128 : (m * 5 + v + 1) * 128, :].astype(F32).T.astype(BF16)
            for xq in range(2):
                table[(v * 2 + m) * 64 : (v * 2 + m + 1) * 64, xq * 128 : xq * 128 + 128] = block[xq * 64 : xq * 64 + 64]
    index = lax.broadcasted_iota(jnp.int32, (64, 128), 0)
    got[...] = jnp.dot(table[...], onehot[OWN], preferred_element_type=F32)

    def body(r, lanes):
        row = cell[OWN, r, :]
        key = (row >> 14) * 64 + (row & 63)
        for m in range(2):
            acc = jnp.zeros((64, 128), F32)
            for v in range(5):
                acc = jnp.where(index + 64 * v == key, got[(v * 2 + m) * 64 : (v * 2 + m + 1) * 64, lanes], acc)
            po[OWN, m, r, :] = jnp.sum(acc, axis=0, keepdims=True)

    table_rows(body)


def observe(field, left, cell, onehot, got, po, out):
    for m in range(2):
        for xq in range(2):
            hi, lo = halves(field[xq * 64 : xq * 64 + 64, m * 128 : m * 128 + 128])
            left[m * 128 : m * 128 + 64, xq * 128 : xq * 128 + 128] = hi
            left[m * 128 + 64 : m * 128 + 128, xq * 128 : xq * 128 + 128] = lo
    index = lax.broadcasted_iota(jnp.int32, (64, 128), 0)
    got[0:256, :] = jnp.dot(left[...], onehot[OWN], preferred_element_type=F32)

    def body(r, lanes):
        total = po[OWN, 0, r, :] * (got[0:64, lanes] + got[64:128, lanes])
        total += po[OWN, 1, r, :] * (got[128:192, lanes] + got[192:256, lanes])
        total = jnp.where(index == (cell[OWN, r, :] & 63), total, 0.0)
        out[r, :] = jnp.sum(total, axis=0, keepdims=True)

    return body


def spread(t, q, cell, onehot, po, values, w):
    index = lax.broadcasted_iota(jnp.int32, (64, 128), 0)

    def body(r, lanes):
        mine = index == (cell[t, r, :] & 63)
        for m in range(2):
            value = po[t, m, r, :] * q[r, :]
            hi = value.astype(BF16).astype(F32)
            values[m * 128 : m * 128 + 64, lanes] = jnp.where(mine, hi, 0.0).astype(BF16)
            values[m * 128 + 64 : m * 128 + 128, lanes] = jnp.where(mine, value - hi, 0.0).astype(BF16)

    table_rows(body)
    got = lax.dot_general(values[...], onehot[t], (((1,), (1,)), ((), ())), preferred_element_type=F32)
    for m in range(2):
        for xq in range(2):
            lanes = slice(xq * 128, xq * 128 + 128)
            w[m * 128 + xq * 64 : m * 128 + xq * 64 + 64, t * 128 : t * 128 + 128] = (
                got[m * 128 : m * 128 + 64, lanes] + got[m * 128 + 64 : m * 128 + 128, lanes]
            )


def spread_edges(t, q, cell, onehot, po, values, edge):
    index = lax.broadcasted_iota(jnp.int32, (8, 128), 0)

    def body(r, lanes):
        column = cell[t, r, :] & 63
        for m in range(2):
            value = po[t, m, r, :] * q[r, :]
            hi = value.astype(BF16).astype(F32)
            for side in range(2):
                mine = index + 56 * side == column
                both = jnp.concatenate([jnp.where(mine, hi, 0.0), jnp.where(mine, value - hi, 0.0)], axis=0)
                values[side * 32 + m * 16 : side * 32 + m * 16 + 16, lanes] = both.astype(BF16)

    table_rows(body)
    got = lax.dot_general(values[...], onehot[t], (((1,), (1,)), ((), ())), preferred_element_type=F32)
    for side in range(2):
        for m in range(2):
            block = got[side * 32 + m * 16 : side * 32 + m * 16 + 16, side * 128 : side * 128 + 128]
            edge[side, m * 8 : m * 8 + 8, t * 128 : t * 128 + 128] = block[0:8] + block[8:16]


def member_part(field, pert, out):
    turned = [field[:, m * 128 : m * 128 + 128].T for m in range(2)]
    for v in range(5):
        block = sum(pert[(m * 5 + v) * 128 : (m * 5 + v + 1) * 128, :].astype(F32) * turned[m] for m in range(2))
        for j in range(MEM):
            out[j, v] = block[j * 16 : j * 16 + 16]


def kernel(
    pert_in, ctrl_in, back_in, cell_in, flag_in, innov_in, prec_in, ky_in, kvo_in, kvh_in, kxo_in, kxs_in, sel_in,
    inc_out, state_out,
    pert, ctrl, back, cell, flag, innov, prec, ky, kvo, kvh, kxo, kxs, sel,
    onehot, table, left, values, edge_values, got, po, q, w, exch, part, edges, fields,
    v_pack, v_edge, v_rows, v_strip, h_send, h_recv, h_recv_b, w_send, w_recv, g_send, g_recv, r_send, r_recv,
    local_sem, send_sem, recv_sem, far_sem,
):
    me_m, me_y, me_x = lax.axis_index("mem"), lax.axis_index("gy"), lax.axis_index("gx")
    up, dn = {"gy": lax.rem(me_y + 3, GY)}, {"gy": lax.rem(me_y + 1, GY)}
    lf, rt = {"gx": lax.rem(me_x + 15, GX)}, {"gx": lax.rem(me_x + 1, GX)}

    def member_peer(i):
        return {"mem": lax.rem(me_m + i, MEM)}

    place = jnp.where(me_x == 0, 0, jnp.where(me_x == GX - 1, 2, 1))
    loads = [
        (ctrl_in, ctrl),
        (sel_in, sel),
        (cell_in, cell.at[OWN]),
        (pert_in, pert),
        (kvo_in.at[me_y], kvo),
        (kvh_in.at[me_y], kvh),
        (kxo_in.at[place], kxo),
        (kxs_in.at[place], kxs),
        (flag_in, flag.at[OWN]),
        (innov_in, innov.at[OWN]),
        (prec_in, prec.at[OWN]),
        (ky_in.at[me_y], ky),
        (back_in, back),
    ]
    loads = [pltpu.make_async_copy(src, dst, local_sem.at[i]) for i, (src, dst) in enumerate(loads)]
    for load in loads:
        load.start()

    barrier = pltpu.get_barrier_semaphore()
    for device in (up, dn, lf, rt, {**up, **lf}, {**up, **rt}, {**dn, **lf}, {**dn, **rt}):
        pl.semaphore_signal(barrier, inc=1, device_id=device, device_id_type=MESH)
    for i in range(1, MEM):
        pl.semaphore_signal(barrier, inc=1, device_id=member_peer(i), device_id_type=MESH)

    sent, sent_all = [], []
    used = [0]

    def copy(src, dst, device):
        i = used[0]
        used[0] += 1
        out = pltpu.make_async_remote_copy(
            src_ref=src, dst_ref=dst, send_sem=send_sem.at[i], recv_sem=recv_sem.at[i], device_id=device, device_id_type=MESH
        )
        out.start()
        sent.append(out)
        return out

    def up_and_dn(ref):
        return [copy(ref.at[OWN], ref.at[DN], up), copy(ref.at[OWN], ref.at[UP], dn)]

    def to_members(source, into):
        base = used[0]
        used[0] += 1
        for i in range(1, MEM):
            pltpu.make_async_remote_copy(
                src_ref=source(i),
                dst_ref=into.at[i - 1],
                send_sem=send_sem.at[base],
                recv_sem=recv_sem.at[base],
                device_id=member_peer(i),
                device_id_type=MESH,
            ).start()
        sent_all.append((into, base))
        return pltpu.make_async_copy(into, into, recv_sem.at[base])

    loads[0].wait()
    field = jnp.concatenate([ctrl[0:128, :].T, ctrl[128:256, :].T], axis=1)
    loads[1].wait()
    packed = mm(field, sel[...])
    v_pack[0], v_pack[1] = packed[:, :128], packed[:, 128:]
    for m in range(2):
        v_edge[0, m] = field[0:8, m * 128 : m * 128 + 128]
        v_edge[1, m] = field[120:128, m * 128 : m * 128 + 128]
    loads[2].wait()

    pl.semaphore_wait(barrier, 8 + MEM - 1)

    first, last = pl.ds(0, 8), pl.ds(120, 8)
    halo = [
        copy(v_pack.at[0], v_rows.at[1], up),
        copy(v_pack.at[1], v_rows.at[0], dn),
        copy(v_pack.at[0, first], v_strip.at[RT, 3], {**up, **lf}),
        copy(v_pack.at[0, last], v_strip.at[LF, 3], {**up, **rt}),
        copy(v_pack.at[1, first], v_strip.at[RT, 2], {**dn, **lf}),
        copy(v_pack.at[1, last], v_strip.at[LF, 2], {**dn, **rt}),
        copy(v_edge.at[0], v_strip.at[RT, pl.ds(0, 2)], lf),
        copy(v_edge.at[1], v_strip.at[LF, pl.ds(0, 2)], rt),
    ]
    tables = up_and_dn(cell)

    build_onehot(cell, onehot, OWN)
    loads[3].wait()
    pert_at_obs(pert, table, cell, onehot, got, po)
    tables += up_and_dn(po)

    for load in loads[4:]:
        load.wait()
    rows_v = times_matrix(field, kvo[...])
    for one in halo:
        one.wait_recv()
    for offset in (2, GX - 2):
        pl.semaphore_signal(far_sem.at[0], inc=1, device_id={"gx": lax.rem(me_x + offset, GX)}, device_id_type=MESH)
    for ref in (innov, prec, flag):
        tables += up_and_dn(ref)
    rows_v += times_matrix(jnp.concatenate([v_rows[0], v_rows[1]], axis=1), kvh[...])
    near = [jnp.concatenate([v_strip[side, 0], v_strip[side, 1]], axis=1) for side in (LF, RT)]
    far = [jnp.concatenate([v_strip[side, 2], v_strip[side, 3]], axis=1) for side in (LF, RT)]
    strips = times_matrix(jnp.concatenate(near, axis=0), kvo[...]) + times_matrix(jnp.concatenate(far, axis=0), kvh[...])
    smoothed = matrix_times(kxo[0:128, :], rows_v) + matrix_times(kxs[0:128, :], strips)

    def sum_members(body, phase, norm):
        table_rows(body, 0, 4)
        first_half = to_members(lambda i: h_send.at[phase, pl.ds(0, 16)], h_recv.at[phase])
        h_send[phase, 32:40, :] = norm
        table_rows(body, 4, 8)
        second_half = to_members(lambda i: h_send.at[phase, pl.ds(16, 24)], h_recv_b.at[phase])

        def total():
            first_half.wait()
            one = h_send[phase, 0:16, :]
            for i in range(MEM - 1):
                one += h_recv[phase, i]
            second_half.wait()
            two = h_send[phase, 16:40, :]
            for i in range(MEM - 1):
                two += h_recv_b[phase, i]
            return jnp.concatenate([one, two[0:16]], axis=0), two[16:24]

        return total

    def levels_total(k):
        out = r_send[k, me_m]
        for i in range(MEM - 1):
            out += r_recv[k, i]
        return out

    total = sum_members(observe(smoothed, left, cell, onehot, got, po, h_send.at[0]), 0, jnp.zeros((8, 128), F32))
    for one in tables[0:2]:
        one.wait_recv()
    build_onehot(cell, onehot, UP)
    build_onehot(cell, onehot, DN)
    exch[0, OWN] = total()[0]
    around = up_and_dn(exch.at[0])
    pl.semaphore_wait(far_sem.at[0], 2)
    for offset in (4, GX - 4):
        pl.semaphore_signal(far_sem.at[1], inc=1, device_id={"gx": lax.rem(me_x + offset, GX)}, device_id_type=MESH)
    state = field
    lane = lax.broadcasted_iota(jnp.int32, (1, 128), 1)
    levels = []

    def terms(t, seen):
        misfit = seen - innov[t]
        weight = jnp.where(flag[t] == 1, 1.0 / jnp.sqrt(1.0 + misfit * misfit), 1.0)
        inverse = prec[t] * weight
        q[t] = inverse * misfit
        return inverse

    def x_stage(along, rows):
        return [
            jnp.concatenate([along[0:rows, k * 128 : k * 128 + 128], along[rows : 2 * rows, k * 128 : k * 128 + 128]], axis=1)
            for k in range(2)
        ]

    for it in range(ITERS):
        for t in (OWN, UP, DN):
            if it == 0:
                if t == UP:
                    for one in tables[2:]:
                        one.wait_recv()
                    around[1].wait_recv()
                elif t == DN:
                    around[0].wait_recv()
                seen = exch[0, t]
            else:
                seen = exch[0, t] - step * exch[1, t]
            inverse_t = terms(t, seen)
            if t == OWN:
                inverse = inverse_t
            spread_edges(t, q.at[t], cell, onehot, po, edge_values, w_send.at[it])
            if it == 0 and t == OWN:
                spread(t, q.at[t], cell, onehot, po, values, w)
        sides = [copy(w_send.at[it, 0], w_recv.at[it, RT], lf), copy(w_send.at[it, 1], w_recv.at[it, LF], rt)]
        if it == ITERS - 1:
            member_part(smoothed, pert, r_send.at[0])
            levels.append(to_members(lambda i: r_send.at[0, lax.rem(me_m + i, MEM)], r_recv.at[0]))
        for t in (OWN, UP, DN):
            if it > 0 or t != OWN:
                spread(t, q.at[t], cell, onehot, po, values, w)
        once, twice = x_stage(times_matrix(w[...], ky[...]), 128)
        part[0] = matrix_times(kxo[0:128, :], once)
        part[1] = matrix_times(kxo[128:256, :], twice)
        for one in sides:
            one.wait_recv()
        edge = [w_recv[it, side, m * 8 : m * 8 + 8, :] for m in range(2) for side in (LF, RT)]
        edges[...] = times_matrix(jnp.concatenate(edge, axis=0), ky[...])
        edge_once, edge_twice = x_stage(edges, 16)
        fields[it, 0] = matrix_times(kxs[0:128, :], edge_once)
        fields[it, 1] = matrix_times(kxs[128:256, :], edge_twice)
        grad = state + (part[0] + fields[it, 0])
        change = smoothed + (part[1] + fields[it, 1])
        body = observe(change, left, cell, onehot, got, po, h_send.at[it + 1])
        norm = jnp.sum((grad * grad).reshape(16, 8, 256), axis=0)
        total = sum_members(body, it + 1, norm[:, 0:128] + norm[:, 128:256])
        if it == ITERS - 1:
            member_part(change, pert, r_send.at[1])
            levels.append(to_members(lambda i: r_send.at[1, lax.rem(me_m + i, MEM)], r_recv.at[1]))
        delta, norm = total()
        norm = jnp.sum(norm, axis=0, keepdims=True)
        curv = jnp.sum(inverse * delta * delta, axis=0, keepdims=True)
        norm = norm + pltpu.roll(norm, 64, 1)
        curv = curv + pltpu.roll(curv, 64, 1)
        both = jnp.where(lane < 64, norm, curv)
        g_send[it] = both
        if it == 0:
            pl.semaphore_wait(far_sem.at[1], 2)
        base = used[0]
        used[0] += 1

        for i, (rows, cols) in enumerate(FAR_FIRST):
            pltpu.make_async_remote_copy(
                src_ref=g_send.at[it],
                dst_ref=g_recv.at[it, i],
                send_sem=send_sem.at[base],
                recv_sem=recv_sem.at[base],
                device_id={"gy": lax.rem(me_y + rows, GY), "gx": lax.rem(me_x + cols, GX)},
                device_id_type=MESH,
            ).start()
        sent_all.append((g_recv.at[it], base))
        if it < ITERS - 1:
            exch[it + 1, OWN] = delta
            around = up_and_dn(exch.at[it + 1])
            for one in around:
                one.wait_recv()
        else:
            for one in levels:
                one.wait()
            total_before, total_change = back[...] + levels_total(0), levels_total(1)
            turned = [[x[:, m * 128 : m * 128 + 128].T for m in range(2)] for x in (state, grad)]
        pltpu.make_async_copy(g_recv.at[it], g_recv.at[it], recv_sem.at[base]).wait()
        both = both + jnp.sum(g_recv[it], axis=0)
        norm = jnp.sum(jnp.where(lane < 64, both, 0.0), axis=1, keepdims=True)
        curv = jnp.sum(jnp.where(lane < 64, 0.0, both), axis=1, keepdims=True)
        step = norm / (norm + curv)
        if it < ITERS - 1:
            state = state - step * grad
            smoothed = smoothed - step * change
    inc_out[...] = total_before - step.reshape(1, 1, 1) * total_change
    for m in range(2):
        state_out[m * 128 : m * 128 + 128, :] = turned[0][m] - step * turned[1][m]
    for one in sent:
        one.wait_send()
    for ref, i in sent_all:
        pltpu.make_async_copy(ref, ref, send_sem.at[i]).wait()


def deliver(inc_in, state_in, inc_out, state_out):
    inc_out[...] = inc_in[...]
    state_out[...] = state_in[...]


def per_device(perturbations, control, background, obs_cell, huber_flag, innovation, precision):
    ky, kv = row_matrices()
    kx, sel = column_matrices(), row_selection()
    kxs = np.zeros((3, 256, 128), BF16)
    kxs[:, :, 0:48] = stack(kx[:, :, 128:144], 2)
    args = (
        perturbations.reshape(1280, 128), control.reshape(256, 128), background.reshape(5, 16, 128),
        obs_cell, huber_flag, innovation, precision,
        jnp.asarray(stack(ky, 1)), jnp.asarray(stack(kv[:, :256], 1)), jnp.asarray(stack(kv[:, 256:], 1)),
        jnp.asarray(stack(kx[:, :, :128], 2)), jnp.asarray(kxs), jnp.asarray(sel),
    )
    i32 = jnp.int32
    inc, state = pl.pallas_call(
        kernel,
        out_shape=(jax.ShapeDtypeStruct((5, 16, 128), F32), jax.ShapeDtypeStruct((256, 128), F32)),
        in_specs=[pl.BlockSpec(memory_space=pl.ANY)] * len(args),
        out_specs=(pl.BlockSpec(memory_space=pltpu.VMEM),) * 2,
        scratch_shapes=[
            pltpu.VMEM((1280, 128), BF16),
            pltpu.VMEM((256, 128), F32),
            pltpu.VMEM((5, 16, 128), F32),
            pltpu.VMEM((3, 32, 128), i32),
            pltpu.VMEM((3, 32, 128), i32),
            pltpu.VMEM((3, 32, 128), F32),
            pltpu.VMEM((3, 32, 128), F32),
            pltpu.VMEM((1152, 256), BF16),
            pltpu.VMEM((768, 256), BF16),
            pltpu.VMEM((768, 256), BF16),
            pltpu.VMEM((256, 384), BF16),
            pltpu.VMEM((256, 128), BF16),
            pltpu.VMEM((256, 256), F32),
            pltpu.VMEM((3, 256, 4096), BF16),
            pltpu.VMEM((640, 256), BF16),
            pltpu.VMEM((256, 256), BF16),
            pltpu.VMEM((256, 4096), BF16),
            pltpu.VMEM((64, 4096), BF16),
            pltpu.VMEM((640, 4096), F32),
            pltpu.VMEM((3, 2, 32, 128), F32),
            pltpu.VMEM((3, 32, 128), F32),
            pltpu.VMEM((256, 384), F32),
            pltpu.VMEM((ITERS, 3, 32, 128), F32),
            pltpu.VMEM((2, 128, 256), F32),
            pltpu.VMEM((32, 256), F32),
            pltpu.VMEM((ITERS, 2, 128, 256), F32),
            pltpu.VMEM((2, 128, 128), F32),
            pltpu.VMEM((2, 2, 8, 128), F32),
            pltpu.VMEM((2, 128, 128), F32),
            pltpu.VMEM((2, 4, 8, 128), F32),
            pltpu.VMEM((ITERS + 1, 40, 128), F32),
            pltpu.VMEM((ITERS + 1, MEM - 1, 16, 128), F32),
            pltpu.VMEM((ITERS + 1, MEM - 1, 24, 128), F32),
            pltpu.VMEM((ITERS, 2, 16, 384), F32),
            pltpu.VMEM((ITERS, 2, 16, 384), F32),
            pltpu.VMEM((ITERS, 1, 128), F32),
            pltpu.VMEM((ITERS, TILES - 1, 1, 128), F32),
            pltpu.VMEM((2, MEM, 5, 16, 128), F32),
            pltpu.VMEM((2, MEM - 1, 5, 16, 128), F32),
            pltpu.SemaphoreType.DMA((13,)),
            pltpu.SemaphoreType.DMA((40,)),
            pltpu.SemaphoreType.DMA((40,)),
            pltpu.SemaphoreType.REGULAR((2,)),
        ],
        compiler_params=pltpu.CompilerParams(collective_id=0, has_side_effects=True, vmem_limit_bytes=63 * 2**20 + 2**19),
    )(*args)
    inc, state = pl.pallas_call(
        deliver,
        out_shape=(jax.ShapeDtypeStruct(inc.shape, F32), jax.ShapeDtypeStruct(state.shape, F32)),
        in_specs=[pl.BlockSpec(memory_space=pltpu.VMEM)] * 2,
        out_specs=(pl.BlockSpec(memory_space=pltpu.VMEM),) * 2,
        compiler_params=pltpu.CompilerParams(vmem_limit_bytes=63 * 2**20 + 2**19),
    )(inc, state)
    return inc.reshape(background.shape), state.reshape(control.shape)


def solution(mesh):
    grid = P("mem", None, "gy", "gx")
    table = P("gy", "gx")
    return jax.shard_map(
        per_device,
        mesh=mesh,
        in_specs=(P("mem", None, None, "gy", "gx"), grid, P(None, "mem", "gy", "gx"), table, table, table, table),
        out_specs=(P(None, "mem", "gy", "gx"), grid),
        check_vma=False,
    )
```

```python
import functools

import jax
import jax.numpy as jnp
import numpy as np
from jax import lax
from jax.experimental import pallas as pl
from jax.experimental.pallas import tpu as pltpu
from jax.sharding import PartitionSpec as P

MESH = pl.DeviceIdType.MESH
F32, BF16 = jnp.float32, jnp.bfloat16
MEM, GY, GX = 8, 4, 16
TILES = GY * GX
ITERS = 2
FAR_FIRST = sorted(
    ((rows, cols) for rows in range(GY) for cols in range(GX) if rows or cols),
    key=lambda at: -(4 * min(at[0], GY - at[0]) + min(at[1], GX - at[1]) / 4),
)
UP, OWN, DN = 0, 1, 2
LF, RT = 0, 1


def taps():
    offsets = np.arange(-4, 5).astype(np.float32)
    raw = np.exp(-offsets * offsets / np.float32(8.0))
    return (raw / raw.sum()).astype(np.float64)


def one_axis(length):
    weights = taps()
    distance = np.arange(length)[None, :] - np.arange(length)[:, None]
    inside = np.abs(distance) <= 4
    once = np.where(inside, weights[np.clip(distance + 4, 0, 8)], 0.0)
    return once, once @ once


def window(full, first_in, rows, first_out, cols):
    out = np.zeros((rows, cols))
    for i in range(rows):
        if 0 <= first_in + i < full.shape[0]:
            out[i] = full[first_in + i, first_out : first_out + cols]
    return out


def row_matrices():
    once, twice = one_axis(GY * 8)
    eye16, eye32 = np.eye(16), np.eye(32)
    ky = np.zeros((GY, 384, 256))
    kv = np.zeros((GY, 512, 256))
    for g in range(GY):
        for t in range(3):
            first = 8 * (g + t - 1)
            ky[g, t * 128 : t * 128 + 128, :128] = np.kron(eye16, window(once, first, 8, 8 * g, 8))
            ky[g, t * 128 : t * 128 + 128, 128:] = np.kron(eye16, window(twice, first, 8, 8 * g, 8))
        kv[g, :256] = np.kron(eye32, window(once, 8 * g, 8, 8 * g, 8))
        kv[g, 256:384] = np.kron(eye32, window(once, 8 * g - 4, 4, 8 * g, 8))
        kv[g, 384:] = np.kron(eye32, window(once, 8 * g + 8, 4, 8 * g, 8))
    return ky.astype(np.float32), kv.astype(np.float32)


def column_matrices():
    length = 128 * 3
    weights = one_axis(length)
    kx = np.zeros((3, 256, 256))
    for place, first in enumerate((0, 128, 256)):
        for k in range(2):
            rows = slice(k * 128, k * 128 + 128)
            kx[place, rows, :128] = window(weights[k], first, 128, first, 128).T
            kx[place, rows, 128:136] = window(weights[k], first - 8, 8, first, 128).T
            kx[place, rows, 136:144] = window(weights[k], first + 128, 8, first, 128).T
    return kx.astype(np.float32)


def split(matrix):
    hi = matrix.astype(BF16)
    return hi, (matrix - hi.astype(np.float32)).astype(BF16)


def stack(matrix, axis):
    hi, lo = split(matrix)
    return np.concatenate([hi, hi, lo], axis=axis)


def row_selection():
    top = np.kron(np.eye(32), np.eye(8)[:, :4])
    bottom = np.kron(np.eye(32), np.eye(8)[:, 4:])
    return np.concatenate([top, bottom], axis=1).astype(np.float32)


def mm(a, b):
    return jnp.dot(a, b, preferred_element_type=F32, precision=lax.Precision.HIGHEST)


def halves(x):
    hi = x.astype(BF16)
    return hi, (x - hi.astype(F32)).astype(BF16)


def times_matrix(x, stacked):
    hi, lo = halves(x)
    return jnp.dot(jnp.concatenate([hi, lo, hi], axis=1), stacked, preferred_element_type=F32)


def matrix_times(stacked, x):
    hi, lo = halves(x)
    parts = [hi, lo, hi]
    more = stacked.shape[1] - 3 * x.shape[0]
    if more:
        parts.append(jnp.zeros((more, x.shape[1]), BF16))
    return jnp.dot(stacked, jnp.concatenate(parts, axis=0), preferred_element_type=F32)


def table_rows(body, first=0, last=8):
    def four(c, carry):
        for k in range(4):
            body(pl.ds(c * 4 + k, 1), pl.ds(pl.multiple_of(c * 512 + k * 128, 128), 128))
        return carry

    lax.fori_loop(first, last, four, 0)


def build_onehot(cell, onehot, t):
    index = lax.broadcasted_iota(jnp.int32, (256, 128), 0)

    def body(r, lanes):
        row = cell[t, r, :]
        key = ((row & 127) >> 6) * 128 + ((row >> 7) & 127)
        onehot[t, :, lanes] = jnp.where(index == key, 1.0, 0.0).astype(BF16)

    table_rows(body)


def pert_at_obs(pert, table, cell, onehot, got, po):
    for v in range(5):
        for m in range(2):
            block = pert[(m * 5 + v) * 128 : (m * 5 + v + 1) * 128, :].astype(F32).T.astype(BF16)
            for xq in range(2):
                table[(v * 2 + m) * 64 : (v * 2 + m + 1) * 64, xq * 128 : xq * 128 + 128] = block[xq * 64 : xq * 64 + 64]
    index = lax.broadcasted_iota(jnp.int32, (64, 128), 0)
    got[...] = jnp.dot(table[...], onehot[OWN], preferred_element_type=F32)

    def body(r, lanes):
        row = cell[OWN, r, :]
        key = (row >> 14) * 64 + (row & 63)
        for m in range(2):
            acc = jnp.zeros((64, 128), F32)
            for v in range(5):
                acc = jnp.where(index + 64 * v == key, got[(v * 2 + m) * 64 : (v * 2 + m + 1) * 64, lanes], acc)
            po[OWN, m, r, :] = jnp.sum(acc, axis=0, keepdims=True)

    table_rows(body)


def observe(field, left, cell, onehot, got, po, out):
    for m in range(2):
        for xq in range(2):
            hi, lo = halves(field[xq * 64 : xq * 64 + 64, m * 128 : m * 128 + 128])
            left[m * 128 : m * 128 + 64, xq * 128 : xq * 128 + 128] = hi
            left[m * 128 + 64 : m * 128 + 128, xq * 128 : xq * 128 + 128] = lo
    index = lax.broadcasted_iota(jnp.int32, (64, 128), 0)
    got[0:256, :] = jnp.dot(left[...], onehot[OWN], preferred_element_type=F32)

    def body(r, lanes):
        total = po[OWN, 0, r, :] * (got[0:64, lanes] + got[64:128, lanes])
        total += po[OWN, 1, r, :] * (got[128:192, lanes] + got[192:256, lanes])
        total = jnp.where(index == (cell[OWN, r, :] & 63), total, 0.0)
        out[r, :] = jnp.sum(total, axis=0, keepdims=True)

    return body


def spread(t, q, cell, onehot, po, values, w):
    index = lax.broadcasted_iota(jnp.int32, (64, 128), 0)

    def body(r, lanes):
        mine = index == (cell[t, r, :] & 63)
        for m in range(2):
            value = po[t, m, r, :] * q[r, :]
            hi = value.astype(BF16).astype(F32)
            values[m * 128 : m * 128 + 64, lanes] = jnp.where(mine, hi, 0.0).astype(BF16)
            values[m * 128 + 64 : m * 128 + 128, lanes] = jnp.where(mine, value - hi, 0.0).astype(BF16)

    table_rows(body)
    got = lax.dot_general(values[...], onehot[t], (((1,), (1,)), ((), ())), preferred_element_type=F32)
    for m in range(2):
        for xq in range(2):
            lanes = slice(xq * 128, xq * 128 + 128)
            w[m * 128 + xq * 64 : m * 128 + xq * 64 + 64, t * 128 : t * 128 + 128] = (
                got[m * 128 : m * 128 + 64, lanes] + got[m * 128 + 64 : m * 128 + 128, lanes]
            )


def spread_edges(t, q, cell, onehot, po, values, edge):
    index = lax.broadcasted_iota(jnp.int32, (8, 128), 0)

    def body(r, lanes):
        column = cell[t, r, :] & 63
        for m in range(2):
            value = po[t, m, r, :] * q[r, :]
            hi = value.astype(BF16).astype(F32)
            for side in range(2):
                mine = index + 56 * side == column
                both = jnp.concatenate([jnp.where(mine, hi, 0.0), jnp.where(mine, value - hi, 0.0)], axis=0)
                values[side * 32 + m * 16 : side * 32 + m * 16 + 16, lanes] = both.astype(BF16)

    table_rows(body)
    got = lax.dot_general(values[...], onehot[t], (((1,), (1,)), ((), ())), preferred_element_type=F32)
    for side in range(2):
        for m in range(2):
            block = got[side * 32 + m * 16 : side * 32 + m * 16 + 16, side * 128 : side * 128 + 128]
            edge[side, m * 8 : m * 8 + 8, t * 128 : t * 128 + 128] = block[0:8] + block[8:16]


def member_part(field, pert, out):
    turned = [field[:, m * 128 : m * 128 + 128].T for m in range(2)]
    for v in range(5):
        block = sum(pert[(m * 5 + v) * 128 : (m * 5 + v + 1) * 128, :].astype(F32) * turned[m] for m in range(2))
        for j in range(MEM):
            out[j, v] = block[j * 16 : j * 16 + 16]


def kernel(
    pert_in, ctrl_in, back_in, cell_in, flag_in, innov_in, prec_in, ky_in, kvo_in, kvh_in, kxo_in, kxs_in, sel_in,
    inc_out, state_out,
    pert, ctrl, back, cell, flag, innov, prec, ky, kvo, kvh, kxo, kxs, sel,
    onehot, table, left, values, edge_values, got, po, q, w, exch, part, edges, fields,
    v_pack, v_edge, v_rows, v_strip, h_send, h_recv, h_recv_b, w_send, w_recv, g_send, g_recv, r_send, r_recv,
    local_sem, send_sem, recv_sem, far_sem,
):
    me_m, me_y, me_x = lax.axis_index("mem"), lax.axis_index("gy"), lax.axis_index("gx")
    up, dn = {"gy": lax.rem(me_y + 3, GY)}, {"gy": lax.rem(me_y + 1, GY)}
    lf, rt = {"gx": lax.rem(me_x + 15, GX)}, {"gx": lax.rem(me_x + 1, GX)}

    def member_peer(i):
        return {"mem": lax.rem(me_m + i, MEM)}

    place = jnp.where(me_x == 0, 0, jnp.where(me_x == GX - 1, 2, 1))
    loads = [
        (ctrl_in, ctrl),
        (sel_in, sel),
        (cell_in, cell.at[OWN]),
        (pert_in, pert),
        (kvo_in.at[me_y], kvo),
        (kvh_in.at[me_y], kvh),
        (kxo_in.at[place], kxo),
        (kxs_in.at[place], kxs),
        (flag_in, flag.at[OWN]),
        (innov_in, innov.at[OWN]),
        (prec_in, prec.at[OWN]),
        (ky_in.at[me_y], ky),
        (back_in, back),
    ]
    loads = [pltpu.make_async_copy(src, dst, local_sem.at[i]) for i, (src, dst) in enumerate(loads)]
    for load in loads:
        load.start()

    barrier = pltpu.get_barrier_semaphore()
    for device in (up, dn, lf, rt, {**up, **lf}, {**up, **rt}, {**dn, **lf}, {**dn, **rt}):
        pl.semaphore_signal(barrier, inc=1, device_id=device, device_id_type=MESH)
    for i in range(1, MEM):
        pl.semaphore_signal(barrier, inc=1, device_id=member_peer(i), device_id_type=MESH)

    sent, sent_all = [], []
    used = [0]

    def copy(src, dst, device):
        i = used[0]
        used[0] += 1
        out = pltpu.make_async_remote_copy(
            src_ref=src, dst_ref=dst, send_sem=send_sem.at[i], recv_sem=recv_sem.at[i], device_id=device, device_id_type=MESH
        )
        out.start()
        sent.append(out)
        return out

    def up_and_dn(ref):
        return [copy(ref.at[OWN], ref.at[DN], up), copy(ref.at[OWN], ref.at[UP], dn)]

    def to_members(source, into):
        base = used[0]
        used[0] += 1
        for i in range(1, MEM):
            pltpu.make_async_remote_copy(
                src_ref=source(i),
                dst_ref=into.at[i - 1],
                send_sem=send_sem.at[base],
                recv_sem=recv_sem.at[base],
                device_id=member_peer(i),
                device_id_type=MESH,
            ).start()
        sent_all.append((into, base))
        return pltpu.make_async_copy(into, into, recv_sem.at[base])

    loads[0].wait()
    field = jnp.concatenate([ctrl[0:128, :].T, ctrl[128:256, :].T], axis=1)
    loads[1].wait()
    packed = mm(field, sel[...])
    v_pack[0], v_pack[1] = packed[:, :128], packed[:, 128:]
    for m in range(2):
        v_edge[0, m] = field[0:8, m * 128 : m * 128 + 128]
        v_edge[1, m] = field[120:128, m * 128 : m * 128 + 128]
    loads[2].wait()

    pl.semaphore_wait(barrier, 8 + MEM - 1)

    first, last = pl.ds(0, 8), pl.ds(120, 8)
    halo = [
        copy(v_pack.at[0], v_rows.at[1], up),
        copy(v_pack.at[1], v_rows.at[0], dn),
        copy(v_pack.at[0, first], v_strip.at[RT, 3], {**up, **lf}),
        copy(v_pack.at[0, last], v_strip.at[LF, 3], {**up, **rt}),
        copy(v_pack.at[1, first], v_strip.at[RT, 2], {**dn, **lf}),
        copy(v_pack.at[1, last], v_strip.at[LF, 2], {**dn, **rt}),
        copy(v_edge.at[0], v_strip.at[RT, pl.ds(0, 2)], lf),
        copy(v_edge.at[1], v_strip.at[LF, pl.ds(0, 2)], rt),
    ]
    tables = up_and_dn(cell)

    build_onehot(cell, onehot, OWN)
    loads[3].wait()
    pert_at_obs(pert, table, cell, onehot, got, po)
    tables += up_and_dn(po)

    for load in loads[4:]:
        load.wait()
    rows_v = times_matrix(field, kvo[...])
    for one in halo:
        one.wait_recv()
    for offset in (2, GX - 2):
        pl.semaphore_signal(far_sem.at[0], inc=1, device_id={"gx": lax.rem(me_x + offset, GX)}, device_id_type=MESH)
    for ref in (innov, prec, flag):
        tables += up_and_dn(ref)
    rows_v += times_matrix(jnp.concatenate([v_rows[0], v_rows[1]], axis=1), kvh[...])
    near = [jnp.concatenate([v_strip[side, 0], v_strip[side, 1]], axis=1) for side in (LF, RT)]
    far = [jnp.concatenate([v_strip[side, 2], v_strip[side, 3]], axis=1) for side in (LF, RT)]
    strips = times_matrix(jnp.concatenate(near, axis=0), kvo[...]) + times_matrix(jnp.concatenate(far, axis=0), kvh[...])
    smoothed = matrix_times(kxo[0:128, :], rows_v) + matrix_times(kxs[0:128, :], strips)

    def sum_members(body, phase, norm):
        table_rows(body, 0, 4)
        first_half = to_members(lambda i: h_send.at[phase, pl.ds(0, 16)], h_recv.at[phase])
        h_send[phase, 32:40, :] = norm
        table_rows(body, 4, 8)
        second_half = to_members(lambda i: h_send.at[phase, pl.ds(16, 24)], h_recv_b.at[phase])

        def total():
            first_half.wait()
            one = h_send[phase, 0:16, :]
            for i in range(MEM - 1):
                one += h_recv[phase, i]
            second_half.wait()
            two = h_send[phase, 16:40, :]
            for i in range(MEM - 1):
                two += h_recv_b[phase, i]
            return jnp.concatenate([one, two[0:16]], axis=0), two[16:24]

        return total

    def levels_total(k):
        out = r_send[k, me_m]
        for i in range(MEM - 1):
            out += r_recv[k, i]
        return out

    total = sum_members(observe(smoothed, left, cell, onehot, got, po, h_send.at[0]), 0, jnp.zeros((8, 128), F32))
    for one in tables[0:2]:
        one.wait_recv()
    build_onehot(cell, onehot, UP)
    build_onehot(cell, onehot, DN)
    exch[0, OWN] = total()[0]
    around = up_and_dn(exch.at[0])
    pl.semaphore_wait(far_sem.at[0], 2)
    for offset in (4, GX - 4):
        pl.semaphore_signal(far_sem.at[1], inc=1, device_id={"gx": lax.rem(me_x + offset, GX)}, device_id_type=MESH)
    state = field
    lane = lax.broadcasted_iota(jnp.int32, (1, 128), 1)
    levels = []

    def terms(t, seen):
        misfit = seen - innov[t]
        weight = jnp.where(flag[t] == 1, 1.0 / jnp.sqrt(1.0 + misfit * misfit), 1.0)
        inverse = prec[t] * weight
        q[t] = inverse * misfit
        return inverse

    def x_stage(along, rows):
        return [
            jnp.concatenate([along[0:rows, k * 128 : k * 128 + 128], along[rows : 2 * rows, k * 128 : k * 128 + 128]], axis=1)
            for k in range(2)
        ]

    for it in range(ITERS):
        for t in (OWN, UP, DN):
            if it == 0:
                if t == UP:
                    for one in tables[2:]:
                        one.wait_recv()
                    around[1].wait_recv()
                elif t == DN:
                    around[0].wait_recv()
                seen = exch[0, t]
            else:
                seen = exch[0, t] - step * exch[1, t]
            inverse_t = terms(t, seen)
            if t == OWN:
                inverse = inverse_t
            spread_edges(t, q.at[t], cell, onehot, po, edge_values, w_send.at[it])
            if it == 0 and t == OWN:
                spread(t, q.at[t], cell, onehot, po, values, w)
        sides = [copy(w_send.at[it, 0], w_recv.at[it, RT], lf), copy(w_send.at[it, 1], w_recv.at[it, LF], rt)]
        for t in (OWN, UP, DN):
            if it > 0 or t != OWN:
                spread(t, q.at[t], cell, onehot, po, values, w)
        once, twice = x_stage(times_matrix(w[...], ky[...]), 128)
        part[0] = matrix_times(kxo[0:128, :], once)
        part[1] = matrix_times(kxo[128:256, :], twice)
        for one in sides:
            one.wait_recv()
        edge = [w_recv[it, side, m * 8 : m * 8 + 8, :] for m in range(2) for side in (LF, RT)]
        edges[...] = times_matrix(jnp.concatenate(edge, axis=0), ky[...])
        edge_once, edge_twice = x_stage(edges, 16)
        fields[it, 0] = matrix_times(kxs[0:128, :], edge_once)
        fields[it, 1] = matrix_times(kxs[128:256, :], edge_twice)
        grad = state + (part[0] + fields[it, 0])
        change = smoothed + (part[1] + fields[it, 1])
        body = observe(change, left, cell, onehot, got, po, h_send.at[it + 1])
        norm = jnp.sum((grad * grad).reshape(16, 8, 256), axis=0)
        total = sum_members(body, it + 1, norm[:, 0:128] + norm[:, 128:256])
        if it == ITERS - 1:
            member_part(smoothed, pert, r_send.at[0])
            levels.append(to_members(lambda i: r_send.at[0, lax.rem(me_m + i, MEM)], r_recv.at[0]))
            member_part(change, pert, r_send.at[1])
            levels.append(to_members(lambda i: r_send.at[1, lax.rem(me_m + i, MEM)], r_recv.at[1]))
        delta, norm = total()
        norm = jnp.sum(norm, axis=0, keepdims=True)
        curv = jnp.sum(inverse * delta * delta, axis=0, keepdims=True)
        norm = norm + pltpu.roll(norm, 64, 1)
        curv = curv + pltpu.roll(curv, 64, 1)
        both = jnp.where(lane < 64, norm, curv)
        g_send[it] = both
        if it == 0:
            pl.semaphore_wait(far_sem.at[1], 2)
        base = used[0]
        used[0] += 1

        for i, (rows, cols) in enumerate(FAR_FIRST):
            pltpu.make_async_remote_copy(
                src_ref=g_send.at[it],
                dst_ref=g_recv.at[it, i],
                send_sem=send_sem.at[base],
                recv_sem=recv_sem.at[base],
                device_id={"gy": lax.rem(me_y + rows, GY), "gx": lax.rem(me_x + cols, GX)},
                device_id_type=MESH,
            ).start()
        sent_all.append((g_recv.at[it], base))
        if it < ITERS - 1:
            exch[it + 1, OWN] = delta
            around = up_and_dn(exch.at[it + 1])
            for one in around:
                one.wait_recv()
        else:
            for one in levels:
                one.wait()
            total_before, total_change = back[...] + levels_total(0), levels_total(1)
            turned = [[x[:, m * 128 : m * 128 + 128].T for m in range(2)] for x in (state, grad)]
        pltpu.make_async_copy(g_recv.at[it], g_recv.at[it], recv_sem.at[base]).wait()
        both = both + jnp.sum(g_recv[it], axis=0)
        norm = jnp.sum(jnp.where(lane < 64, both, 0.0), axis=1, keepdims=True)
        curv = jnp.sum(jnp.where(lane < 64, 0.0, both), axis=1, keepdims=True)
        step = norm / (norm + curv)
        if it < ITERS - 1:
            state = state - step * grad
            smoothed = smoothed - step * change
    inc_out[...] = total_before - step.reshape(1, 1, 1) * total_change
    for m in range(2):
        state_out[m * 128 : m * 128 + 128, :] = turned[0][m] - step * turned[1][m]
    for one in sent:
        one.wait_send()
    for ref, i in sent_all:
        pltpu.make_async_copy(ref, ref, send_sem.at[i]).wait()


def deliver(inc_in, state_in, inc_out, state_out):
    inc_out[...] = inc_in[...]
    state_out[...] = state_in[...]


def per_device(perturbations, control, background, obs_cell, huber_flag, innovation, precision):
    ky, kv = row_matrices()
    kx, sel = column_matrices(), row_selection()
    kxs = np.zeros((3, 256, 128), BF16)
    kxs[:, :, 0:48] = stack(kx[:, :, 128:144], 2)
    args = (
        perturbations.reshape(1280, 128), control.reshape(256, 128), background.reshape(5, 16, 128),
        obs_cell, huber_flag, innovation, precision,
        jnp.asarray(stack(ky, 1)), jnp.asarray(stack(kv[:, :256], 1)), jnp.asarray(stack(kv[:, 256:], 1)),
        jnp.asarray(stack(kx[:, :, :128], 2)), jnp.asarray(kxs), jnp.asarray(sel),
    )
    i32 = jnp.int32
    inc, state = pl.pallas_call(
        kernel,
        out_shape=(jax.ShapeDtypeStruct((5, 16, 128), F32), jax.ShapeDtypeStruct((256, 128), F32)),
        in_specs=[pl.BlockSpec(memory_space=pl.ANY)] * len(args),
        out_specs=(pl.BlockSpec(memory_space=pltpu.VMEM),) * 2,
        scratch_shapes=[
            pltpu.VMEM((1280, 128), BF16),
            pltpu.VMEM((256, 128), F32),
            pltpu.VMEM((5, 16, 128), F32),
            pltpu.VMEM((3, 32, 128), i32),
            pltpu.VMEM((3, 32, 128), i32),
            pltpu.VMEM((3, 32, 128), F32),
            pltpu.VMEM((3, 32, 128), F32),
            pltpu.VMEM((1152, 256), BF16),
            pltpu.VMEM((768, 256), BF16),
            pltpu.VMEM((768, 256), BF16),
            pltpu.VMEM((256, 384), BF16),
            pltpu.VMEM((256, 128), BF16),
            pltpu.VMEM((256, 256), F32),
            pltpu.VMEM((3, 256, 4096), BF16),
            pltpu.VMEM((640, 256), BF16),
            pltpu.VMEM((256, 256), BF16),
            pltpu.VMEM((256, 4096), BF16),
            pltpu.VMEM((64, 4096), BF16),
            pltpu.VMEM((640, 4096), F32),
            pltpu.VMEM((3, 2, 32, 128), F32),
            pltpu.VMEM((3, 32, 128), F32),
            pltpu.VMEM((256, 384), F32),
            pltpu.VMEM((ITERS, 3, 32, 128), F32),
            pltpu.VMEM((2, 128, 256), F32),
            pltpu.VMEM((32, 256), F32),
            pltpu.VMEM((ITERS, 2, 128, 256), F32),
            pltpu.VMEM((2, 128, 128), F32),
            pltpu.VMEM((2, 2, 8, 128), F32),
            pltpu.VMEM((2, 128, 128), F32),
            pltpu.VMEM((2, 4, 8, 128), F32),
            pltpu.VMEM((ITERS + 1, 40, 128), F32),
            pltpu.VMEM((ITERS + 1, MEM - 1, 16, 128), F32),
            pltpu.VMEM((ITERS + 1, MEM - 1, 24, 128), F32),
            pltpu.VMEM((ITERS, 2, 16, 384), F32),
            pltpu.VMEM((ITERS, 2, 16, 384), F32),
            pltpu.VMEM((ITERS, 1, 128), F32),
            pltpu.VMEM((ITERS, TILES - 1, 1, 128), F32),
            pltpu.VMEM((2, MEM, 5, 16, 128), F32),
            pltpu.VMEM((2, MEM - 1, 5, 16, 128), F32),
            pltpu.SemaphoreType.DMA((13,)),
            pltpu.SemaphoreType.DMA((40,)),
            pltpu.SemaphoreType.DMA((40,)),
            pltpu.SemaphoreType.REGULAR((2,)),
        ],
        compiler_params=pltpu.CompilerParams(collective_id=0, has_side_effects=True, vmem_limit_bytes=63 * 2**20 + 2**19),
    )(*args)
    inc, state = pl.pallas_call(
        deliver,
        out_shape=(jax.ShapeDtypeStruct(inc.shape, F32), jax.ShapeDtypeStruct(state.shape, F32)),
        in_specs=[pl.BlockSpec(memory_space=pltpu.VMEM)] * 2,
        out_specs=(pl.BlockSpec(memory_space=pltpu.VMEM),) * 2,
        compiler_params=pltpu.CompilerParams(vmem_limit_bytes=63 * 2**20 + 2**19),
    )(inc, state)
    return inc.reshape(background.shape), state.reshape(control.shape)


def solution(mesh):
    grid = P("mem", None, "gy", "gx")
    table = P("gy", "gx")
    return jax.shard_map(
        per_device,
        mesh=mesh,
        in_specs=(P("mem", None, None, "gy", "gx"), grid, P(None, "mem", "gy", "gx"), table, table, table, table),
        out_specs=(P(None, "mem", "gy", "gx"), grid),
        check_vma=False,
    )
```
